128 devices in a mesh: tile: 16 (over y, z_lo, core), col: 8 (over z_hi, x).
Axes of the slice: x: 4, y: 4, z: 4 (z_hi: 2, z_lo: 2; z = z_hi * 2 + z_lo), core: 2. Of those that a mesh axis runs over, the one named last changes fastest.
Arguments:
- impedance: bfloat16 [2, 16384, 16384], P(None, 'tile', 'col'), may hold values from -0.0234375 to 0.0234375
- mobility: bfloat16 [256, 64, 128], P('tile'), may hold values from -0.5 to 0.5
- force: bfloat16 [512, 256, 128], P('col', 'tile'), may hold values from -6 to 6
- patch_map: int32 [16384], replicated, may hold values from 0 to 16383, each once
- ownership: int32 [256], P('tile'), may hold values from 0 to 255, each once
Outputs:
- velocity: bfloat16 [512, 256, 128], P('col', 'tile')
- pressure: bfloat16 [512, 2, 16384], P('col', None, 'tile')
The draws below stay inside these ranges and needn't reach their ends.
Inputs may be any that keep to these rules, and one draw needn't show every extreme that they name: `patch_map`: each patch appears exactly once. `ownership`: each panel appears exactly once.
All inputs are finite; a program needn't handle non-finite values.
Results may differ from the reference program's by a relative error of at most 0.018.
Values may be sent and summed in bfloat16 or wider, within the bound.
No kernel may reach another device: no remote copies, remote signals or barrier semaphores. Data moves between devices by JAX's collectives and lax.ppermute only.
A program may use at most 64 MiB of HBM per device.

```python
import jax
import jax.numpy as jnp
from jax import lax

P_SIZE = 16384
K = 64
LOADS = 512
ITERS = 2
PANELS = 256


def level_of(own_key, extent, cuts, smallest, high):
    def one(dim, blocks):
        steps = jax.random.uniform(jax.random.fold_in(jax.random.fold_in(own_key, 6), dim), (blocks,), jnp.float32, smallest / len(cuts), high / len(cuts))
        return jnp.repeat(jnp.exp(steps), extent[dim] // blocks).reshape((-1,) + (1,) * (len(extent) - dim - 1))

    factor_of = one(*cuts[0])
    for cut in cuts[1:]:
        factor_of = factor_of * one(*cut)
    return factor_of


def centred(own_key, shape, width, most, cuts=(), held_as=jnp.bfloat16):
    level = level_of(own_key, shape, cuts, -0.22, 0.18) if cuts else 1.0
    entries = jax.random.normal(own_key, shape, jnp.float32) * width * level
    return jnp.minimum(jnp.maximum(entries, -most), most).astype(held_as)


def setup_inputs(seed: int = 0) -> dict:
    key_list = jax.random.split(jax.random.key(seed), 6)
    return {
        "impedance": centred(key_list[0], (2, P_SIZE, P_SIZE), (4 * P_SIZE) ** -0.5, 0.0234375, ((1, 16), (2, 8))),
        "mobility": centred(key_list[1], (PANELS, K, 2 * K), (2 * K) ** -0.5, 0.5, ((0, 16),)),
        "force": centred(key_list[2], (LOADS, PANELS, 2 * K), 1.0, 6.0, ((0, 8), (1, 16))),
        "patch_map": jax.random.permutation(key_list[3], P_SIZE).astype(jnp.int32),
        "ownership": jax.random.permutation(key_list[4], PANELS).astype(jnp.int32),
    }


def impedance_product(impedance, field):
    highest = lax.Precision.HIGHEST
    vel_re = field[:, 0].astype(jnp.float32)
    vel_im = field[:, 1].astype(jnp.float32)
    rows_block = P_SIZE // 16

    def one_block(block_index):
        z_block = lax.dynamic_slice_in_dim(impedance, block_index * rows_block, rows_block, 1).astype(jnp.float32)
        real_part = jnp.dot(vel_re, z_block[0].T, precision=highest) - jnp.dot(vel_im, z_block[1].T, precision=highest)
        imag_part = jnp.dot(vel_re, z_block[1].T, precision=highest) + jnp.dot(vel_im, z_block[0].T, precision=highest)
        return jnp.stack([real_part, imag_part], 1)

    blocks = lax.map(one_block, jnp.arange(16, dtype=jnp.int32))
    return jnp.transpose(blocks, (1, 2, 0, 3)).reshape(LOADS, 2, P_SIZE)


def panel_response(drive, mobility):
    highest = lax.Precision.HIGHEST
    drive_f = drive.astype(jnp.float32)
    mob_f = mobility.astype(jnp.float32)
    drive_re = drive_f[..., :K]
    drive_im = drive_f[..., K:]
    mob_re = mob_f[:, :, :K]
    mob_im = mob_f[:, :, K:]
    out_re = jnp.einsum("lsk,sjk->lsj", drive_re, mob_re, precision=highest) - jnp.einsum("lsk,sjk->lsj", drive_im, mob_im, precision=highest)
    out_im = jnp.einsum("lsk,sjk->lsj", drive_re, mob_im, precision=highest) + jnp.einsum("lsk,sjk->lsj", drive_im, mob_re, precision=highest)
    return jnp.concatenate([out_re, out_im], -1).astype(jnp.bfloat16)


def reference(impedance, mobility, force, patch_map, ownership):
    slot_patches = patch_map.reshape(P_SIZE // K, K)[ownership].reshape(P_SIZE).astype(jnp.int32)

    def to_natural(velocity_slots):
        values = velocity_slots.reshape(LOADS, P_SIZE // K, 2, K).transpose(0, 2, 1, 3).reshape(LOADS, 2, P_SIZE)
        return jnp.zeros((LOADS, 2, P_SIZE), jnp.bfloat16).at[:, :, slot_patches].set(values)

    def from_natural(field):
        return field[:, :, slot_patches].reshape(LOADS, 2, P_SIZE // K, K).transpose(0, 2, 1, 3).reshape(LOADS, P_SIZE // K, 2 * K)

    velocity = panel_response(force, mobility)
    pressure = jnp.zeros((LOADS, 2, P_SIZE), jnp.bfloat16)
    for iteration in range(ITERS):
        pressure = impedance_product(impedance, to_natural(velocity)).astype(jnp.bfloat16)
        drive = (force.astype(jnp.float32) - from_natural(pressure).astype(jnp.float32)).astype(jnp.bfloat16)
        velocity = panel_response(drive, mobility)
    return velocity, pressure
```

```python
import functools

import jax
import jax.numpy as jnp
from jax import lax
from jax.experimental import pallas as pl
from jax.experimental.pallas import tpu as pltpu
from jax.sharding import PartitionSpec as P

ITERS = 2
BLOCK = 128
CAP = 112
BF16 = jnp.bfloat16
F32 = jnp.float32
I32 = jnp.int32


def vmem(n):
    return [pl.BlockSpec(memory_space=pltpu.VMEM)] * n


def params(mib):
    return pltpu.CompilerParams(vmem_limit_bytes=mib * 1024 * 1024)


def dot(a, b):
    return jnp.dot(a, b, preferred_element_type=F32)


def onehot(cond):
    return jnp.where(cond, 1.0, 0.0).astype(BF16)


def turned(x):
    half = x.shape[-1] // 2
    rolled = pltpu.roll(x, half, x.ndim - 1)
    lane = lax.broadcasted_iota(I32, x.shape, x.ndim - 1)
    return jnp.where(lane < half, -rolled, rolled)


def respond(mob_ref, drive_ref, out_ref, slots, width):
    for s in range(slots):
        d = drive_ref[s * width:(s + 1) * width, :]
        t = turned(d.astype(F32)).astype(BF16)
        both = jnp.concatenate([d, t], 0)
        out_ref[s * width:(s + 1) * width, :] = dot(mob_ref[s], both).astype(BF16)


def ranks(dest_col, dest_row, groups):
    n = dest_col.shape[0]
    r0 = lax.broadcasted_iota(I32, (n, n), 0)
    r1 = lax.broadcasted_iota(I32, (n, n), 1)
    one_c = onehot(lax.broadcasted_iota(I32, (n, 128), 1) == dest_col)
    cum_c = dot(onehot(r1 < r0), one_c)
    rank_c = jnp.sum(cum_c * one_c.astype(F32), 1, keepdims=True)
    one_r = onehot(lax.broadcasted_iota(I32, (groups, n), 0) == dest_row)
    cum_r = dot(one_r, onehot(r0 < r1))
    rank_r = jnp.sum(cum_r * one_r.astype(F32), 0, keepdims=True)
    most = jnp.max(jnp.sum(one_r.astype(F32), 1))
    return rank_c.astype(I32), rank_r.astype(I32), most


def code_of(dest, rank):
    return jnp.where(rank < CAP, dest * BLOCK + rank, -1)


def pack_rows(code_row, rows, out_ref, groups):
    n = rows.shape[0]
    for d in range(0, groups, 2):
        j = lax.broadcasted_iota(I32, (2 * BLOCK, n), 0) + d * BLOCK
        out_ref[d * BLOCK:(d + 2) * BLOCK, :] = dot(onehot(j == code_row), rows).astype(BF16)


def start_kernel(groups, col_tiles, slots, width, pc_ref, pr_ref, force_ref, mob_ref, buf_ref, code_a_ref, code_d_ref, vel):
    pc, pr = pc_ref[...], pr_ref[...]
    n = pc.shape[0]
    col_width = n * groups // col_tiles

    def dest_a(p):
        return (p % col_width) // BLOCK

    def local_a(p):
        return (p // col_width) * BLOCK + p % BLOCK

    rca, rra, most_a = ranks(dest_a(pc), dest_a(pr), groups)
    rcd, _, most_d = ranks(pc // n, pr // n, groups)
    code_a_col = code_of(dest_a(pc), rca)
    code_a_row = code_of(dest_a(pr), rra)
    code_d_col = code_of(pc // n, rcd)
    code_a_ref[...] = code_a_row
    code_d_ref[...] = code_d_col
    respond(mob_ref, force_ref, vel, slots, width)
    pack_rows(code_a_row, vel[...], buf_ref, groups)
    na = local_a(pr) + 1
    nd = pr % n + 1
    row16 = lax.broadcasted_iota(I32, (16, n), 0)
    va = jnp.where(row16 == 0, na // 256, jnp.where(row16 == 1, na % 256, 0)).astype(F32).astype(BF16)
    vd = jnp.where(row16 == 2, nd // 256, jnp.where(row16 == 3, nd % 256, 0)).astype(F32).astype(BF16)
    most = jnp.maximum(most_a, most_d)
    over = jnp.where(most > CAP, 1.0, 0.0)
    last = lax.broadcasted_iota(I32, (16, BLOCK), 0) == 4
    for d in range(groups):
        j = lax.broadcasted_iota(I32, (n, BLOCK), 1) + d * BLOCK
        aux = dot(va, onehot(j == code_a_col)) + dot(vd, onehot(j == code_d_col))
        aux = jnp.where(last, over, aux)
        buf_ref[d * BLOCK + CAP:(d + 1) * BLOCK, :] = aux.astype(BF16)


def index_kernel(groups, buf_ref, na_ref, nd_ref, over_ref):
    over = jnp.zeros((1, BLOCK), F32)
    for d in range(groups):
        aux = buf_ref[d * BLOCK + CAP:(d + 1) * BLOCK, :].astype(F32)
        na_ref[d:d + 1, :] = (aux[0:1] * 256 + aux[1:2]).astype(I32) - 1
        nd_ref[d:d + 1, :] = (aux[2:3] * 256 + aux[3:4]).astype(I32) - 1
        over = jnp.maximum(over, aux[4:5])
    over_ref[...] = over.astype(I32)


def unpack_kernel(groups, na_ref, buf_ref, out_ref):
    n = out_ref.shape[0]
    total = jnp.zeros(out_ref.shape, F32)
    for d in range(0, groups, 2):
        idx = jnp.concatenate([na_ref[d:d + 1, :], na_ref[d + 1:d + 2, :]], 1)
        pick = onehot(lax.broadcasted_iota(I32, (n, 2 * BLOCK), 0) == idx)
        total += dot(pick, buf_ref[d * BLOCK:(d + 2) * BLOCK, :])
    out_ref[...] = total.astype(BF16)


def product_kernel(z_ref, g_ref, out_ref, f_ref):
    tiles, blocks, rows, _ = g_ref.shape
    depth = tiles * rows

    @pl.when(pl.program_id(0) == 0)
    def _():
        for t in range(tiles):
            for b in range(blocks):
                x = g_ref[t, b]
                f_ref[t * rows:(t + 1) * rows, b * 128:(b + 1) * 128] = x
                f_ref[depth + t * rows:depth + (t + 1) * rows, b * 128:(b + 1) * 128] = turned(x.astype(F32)).astype(BF16)

    for b in range(0, blocks, 2):
        lanes = slice(b * 128, (b + 2) * 128)
        r = dot(z_ref[0], f_ref[:depth, lanes]) + dot(z_ref[1], f_ref[depth:, lanes])
        r = r.astype(BF16)
        out_ref[b] = r[:, :128]
        out_ref[b + 1] = r[:, 128:]


def pressure_kernel(groups, part_ref, ndc_ref, p_ref, buf_ref):
    total = part_ref[0].astype(F32)
    for b in range(1, part_ref.shape[0]):
        total += part_ref[b].astype(F32)
    p = total.astype(BF16)
    p_ref[...] = p
    n = p.shape[0]
    for d in range(0, groups, 2):
        idx = ndc_ref[d * BLOCK:(d + 2) * BLOCK, :]
        pick = onehot(lax.broadcasted_iota(I32, (2 * BLOCK, n), 1) == idx)
        buf_ref[d * BLOCK:(d + 2) * BLOCK, :] = dot(pick, p).astype(BF16)


def response_kernel(groups, slots, width, pack, buf_ref, force_ref, mob_ref, code_d_ref, code_a_ref, out_ref, drive, vel):
    n = force_ref.shape[0]
    total = jnp.zeros(force_ref.shape, F32)
    for d in range(0, groups, 2):
        j = lax.broadcasted_iota(I32, (n, 2 * BLOCK), 1) + d * BLOCK
        total += dot(onehot(j == code_d_ref[...]), buf_ref[d * BLOCK:(d + 2) * BLOCK, :])
    drive[...] = (force_ref[...].astype(F32) - total).astype(BF16)
    if pack:
        respond(mob_ref, drive, vel, slots, width)
        pack_rows(code_a_ref[...], vel[...], out_ref, groups)
    else:
        respond(mob_ref, drive, out_ref, slots, width)


def any_order(impedance, mobility, force, patch_map, ownership):
    imp_re = impedance[0]
    imp_im = impedance[1]
    panel_width = mobility.shape[1]
    slot_count = mobility.shape[0]
    patch_count = patch_map.shape[0]
    loads_dev = force.shape[0]
    col_width = patch_count // lax.axis_size("col")
    row_width = imp_re.shape[0]
    col_index = lax.axis_index("col")
    slot_flat = patch_map.reshape(-1, panel_width)[ownership].reshape(slot_count * panel_width)
    mob_re_t = jnp.transpose(mobility[:, :, :panel_width], (0, 2, 1))
    mob_im_t = jnp.transpose(mobility[:, :, panel_width:], (0, 2, 1))
    upper_rows = jnp.concatenate([mob_re_t, mob_im_t], 2)
    lower_rows = jnp.concatenate([-mob_im_t, mob_re_t], 2)
    real_form = jnp.concatenate([upper_rows, lower_rows], 1)

    def panel_response(drive):
        return jnp.einsum("lsk,skj->lsj", drive, real_form, preferred_element_type=F32).astype(BF16)

    velocity = panel_response(force)
    pressure = jnp.zeros((loads_dev, 2, row_width), BF16)
    for iteration in range(ITERS):
        all_loads = lax.all_gather(velocity, "col", axis=0, tiled=True)
        load_total = all_loads.shape[0]
        values = (
            all_loads.reshape(load_total, slot_count, 2, panel_width)
            .transpose(0, 2, 1, 3)
            .reshape(load_total, 2, slot_count * panel_width)
        )
        local_pos = slot_flat - col_index * col_width
        inside = (local_pos >= 0) & (local_pos < col_width)
        target = jnp.where(inside, local_pos, col_width)
        placed = jnp.zeros((load_total, 2, col_width), BF16).at[:, :, target].set(values, mode="drop")
        columns = lax.psum(placed, "tile").reshape(load_total, 2 * col_width)
        vel_re = columns[:, :col_width]
        vel_im = columns[:, col_width:]

        def dot_rows(left, right):
            return lax.dot_general(left, right, (((1,), (1,)), ((), ())), preferred_element_type=F32)

        real_part = dot_rows(vel_re, imp_re) - dot_rows(vel_im, imp_im)
        imag_part = dot_rows(vel_re, imp_im) + dot_rows(vel_im, imp_re)
        pressure = lax.psum_scatter(
            jnp.concatenate([real_part, imag_part], 1).astype(BF16), "col", scatter_dimension=0, tiled=True
        ).reshape(loads_dev, 2, row_width)
        gathered = lax.all_gather(pressure, "tile", axis=2, tiled=True)
        picked = (
            gathered[:, :, slot_flat]
            .reshape(loads_dev, 2, slot_count, panel_width)
            .transpose(0, 2, 1, 3)
            .reshape(loads_dev, slot_count, 2 * panel_width)
        )
        drive = (force.astype(F32) - picked.astype(F32)).astype(BF16)
        velocity = panel_response(drive)
    return velocity, pressure


def per_device(impedance, mobility, force, patch_map, ownership):
    slots, width, _ = mobility.shape
    loads = force.shape[0]
    groups = lax.axis_size("tile")
    col_tiles = lax.axis_size("col")
    n = slots * width
    depth = impedance.shape[2]
    rows = groups * BLOCK
    patches = patch_map.reshape(-1, width)[ownership].reshape(n)
    force_t = force.reshape(loads, slots, 2, width).transpose(1, 3, 2, 0).reshape(n, 2 * loads)

    def exchange(buf, axis):
        k = lax.axis_size(axis)
        return lax.all_to_all(buf.reshape(k, -1, buf.shape[-1]), axis, 0, 0).reshape(buf.shape)

    def sds(*shape, dtype=BF16):
        return jax.ShapeDtypeStruct(shape, dtype)

    buf, code_a, code_d = pl.pallas_call(
        functools.partial(start_kernel, groups, col_tiles, slots, width),
        out_shape=(sds(rows, 2 * loads), sds(1, n, dtype=I32), sds(n, 1, dtype=I32)),
        in_specs=vmem(4),
        out_specs=tuple(vmem(3)),
        scratch_shapes=[pltpu.VMEM((n, 2 * loads), BF16)],
        compiler_params=params(40),
        name="start",
    )(patches[:, None], patches[None, :], force_t, mobility)
    buf = exchange(buf, "tile")
    na, nd, over = pl.pallas_call(
        functools.partial(index_kernel, groups),
        out_shape=(sds(groups, BLOCK, dtype=I32), sds(groups, BLOCK, dtype=I32), sds(1, BLOCK, dtype=I32)),
        in_specs=vmem(1),
        out_specs=tuple(vmem(3)),
        name="positions",
    )(buf)

    def balanced():
        nd_col = nd.reshape(rows, 1)
        received = buf
        for iteration in range(ITERS):
            natural = pl.pallas_call(
                functools.partial(unpack_kernel, groups),
                out_shape=sds(n, 2 * loads),
                in_specs=vmem(2),
                out_specs=vmem(1)[0],
                compiler_params=params(32),
                name="unpack",
            )(na, received)
            mine = lax.all_to_all(natural.reshape(col_tiles, BLOCK, 2 * loads), "col", 0, 0)
            field = lax.all_gather(mine, "tile", axis=0)
            steps = 2
            part = pl.pallas_call(
                product_kernel,
                out_shape=sds(col_tiles, n, 2 * loads),
                grid=(steps,),
                in_specs=[
                    pl.BlockSpec((2, n // steps, depth), lambda i: (0, i, 0)),
                    pl.BlockSpec(memory_space=pltpu.VMEM),
                ],
                out_specs=pl.BlockSpec((col_tiles, n // steps, 2 * loads), lambda i: (0, i, 0)),
                scratch_shapes=[pltpu.VMEM((2 * depth, col_tiles * 2 * loads), BF16)],
                compiler_params=params(48),
                name="product",
            )(impedance, field)
            part = lax.all_to_all(part, "col", 0, 0)
            pressure, out = pl.pallas_call(
                functools.partial(pressure_kernel, groups),
                out_shape=(sds(n, 2 * loads), sds(rows, 2 * loads)),
                in_specs=vmem(2),
                out_specs=tuple(vmem(2)),
                compiler_params=params(40),
                name="pressure",
            )(part, nd_col)
            back = exchange(out, "tile")
            pack = iteration < ITERS - 1
            velocity = pl.pallas_call(
                functools.partial(response_kernel, groups, slots, width, pack),
                out_shape=sds(rows if pack else n, 2 * loads),
                in_specs=vmem(5),
                out_specs=vmem(1)[0],
                scratch_shapes=[pltpu.VMEM((n, 2 * loads), BF16), pltpu.VMEM((n, 2 * loads), BF16)],
                compiler_params=params(40),
                name="response",
            )(back, force_t, mobility, code_d, code_a)
            if pack:
                received = exchange(velocity, "tile")
        velocity = velocity.reshape(slots, width, 2, loads).transpose(3, 0, 2, 1).reshape(loads, slots, 2 * width)
        pressure = pressure.reshape(n, 2, loads).transpose(2, 1, 0)
        return velocity, pressure

    def unbalanced():
        return any_order(impedance, mobility, force, patch_map, ownership)

    return lax.cond(over[0, 0] == 0, balanced, unbalanced)


def solution(mesh):
    return jax.shard_map(
        per_device,
        mesh=mesh,
        in_specs=(
            P(None, "tile", "col"),
            P("tile", None, None),
            P("col", "tile", None),
            P(),
            P("tile"),
        ),
        out_specs=(P("col", "tile", None), P("col", None, "tile")),
        check_vma=False,
    )
```

```python
import functools

import jax
import jax.numpy as jnp
from jax import lax
from jax.experimental import pallas as pl
from jax.experimental.pallas import tpu as pltpu
from jax.sharding import Mesh
from jax.sharding import PartitionSpec as P

ITERS = 2
LANES = 128
USUAL = 128
LARGEST = 1152
BF16 = jnp.bfloat16
F32 = jnp.float32
I32 = jnp.int32


def vmem(n):
    return [pl.BlockSpec(memory_space=pltpu.VMEM)] * n


def params(mib):
    return pltpu.CompilerParams(vmem_limit_bytes=mib * 1024 * 1024)


def dot(a, b):
    return jnp.dot(a, b, preferred_element_type=F32)


def onehot(cond):
    return jnp.where(cond, 1.0, 0.0).astype(BF16)


def turned(x):
    half = x.shape[-1] // 2
    rolled = pltpu.roll(x, half, x.ndim - 1)
    lane = lax.broadcasted_iota(I32, x.shape, x.ndim - 1)
    return jnp.where(lane < half, -rolled, rolled)


def respond(mob_ref, drive_ref, out_ref, slots, width):
    for s in range(slots):
        d = drive_ref[s * width:(s + 1) * width, :]
        t = turned(d.astype(F32)).astype(BF16)
        both = jnp.concatenate([d, t], 0)
        out_ref[s * width:(s + 1) * width, :] = dot(mob_ref[s], both).astype(BF16)


def ranks(dest_col, dest_row, groups):
    n = dest_col.shape[0]
    r0 = lax.broadcasted_iota(I32, (n, n), 0)
    r1 = lax.broadcasted_iota(I32, (n, n), 1)
    one_c = onehot(lax.broadcasted_iota(I32, (n, 128), 1) == dest_col)
    cum_c = dot(onehot(r1 < r0), one_c)
    rank_c = jnp.sum(cum_c * one_c.astype(F32), 1, keepdims=True)
    one_r = onehot(lax.broadcasted_iota(I32, (groups, n), 0) == dest_row)
    cum_r = dot(one_r, onehot(r0 < r1))
    rank_r = jnp.sum(cum_r * one_r.astype(F32), 0, keepdims=True)
    most = jnp.max(jnp.sum(one_r.astype(F32), 1))
    return rank_c.astype(I32), rank_r.astype(I32), most


def aux_rows(block):
    return -(-(4 * block // LANES + 1) // 16) * 16


def capacity(block):
    return block - aux_rows(block)


def each(count, body):
    if count <= 16:
        for i in range(count):
            body(i)
    else:
        pl.loop(0, count)(body)


def at(start, size):
    if isinstance(start, int):
        return slice(start, start + size)
    return pl.ds(pl.multiple_of(start, 128), size)


def code_of(dest, rank, block):
    return jnp.where(rank < capacity(block), dest * block + rank, -1)


def pack_rows(code_row, rows, out_ref):
    n = rows.shape[0]
    step = 256

    def body(i):
        j = lax.broadcasted_iota(I32, (step, n), 0) + i * step
        out_ref[at(i * step, step), :] = dot(onehot(j == code_row), rows).astype(BF16)

    each(out_ref.shape[0] // step, body)


def to_rows(in_ref, out_ref, stage, slots, width):
    stage[...] = in_ref[...].astype(F32)
    loads = in_ref.shape[0] // slots
    for s in range(slots):
        x = stage[pl.ds(s, loads, stride=slots), :].T
        out_ref[s * width:(s + 1) * width, :] = jnp.concatenate([x[:width], x[width:]], 1).astype(BF16)


def from_rows(rows, out_ref, stage, slots, width):
    loads = out_ref.shape[0] // slots
    for s in range(slots):
        x = rows[s * width:(s + 1) * width, :].astype(F32)
        x = jnp.concatenate([x[:, :loads], x[:, loads:]], 0).T
        stage[pl.ds(s, loads, stride=slots), :] = x
    out_ref[...] = stage[...].astype(BF16)


def start_kernel(groups, col_tiles, slots, width, block, pc_ref, pr_ref, loads_ref, mob_ref, z_ref, buf_ref, code_a_ref, code_d_ref, force_ref, held_ref, vel, aux_ref, stage, sem):
    hold = pltpu.make_async_copy(z_ref, held_ref, sem)
    hold.start()
    to_rows(loads_ref, force_ref, stage, slots, width)
    pc, pr = pc_ref[...], pr_ref[...]
    n = pc.shape[0]
    col_width = n * groups // col_tiles
    chunk = n // col_tiles
    cap = capacity(block)

    def dest_a(p):
        q = (p % col_width) // chunk
        return (q % (groups // 2)) * 2 + q // (groups // 2)

    def local_a(p):
        return (p // col_width) * chunk + p % chunk

    rca, rra, most_a = ranks(dest_a(pc), dest_a(pr), groups)
    rcd, _, most_d = ranks(pc // n, pr // n, groups)
    code_a_col = code_of(dest_a(pc), rca, block)
    code_a_row = code_of(dest_a(pr), rra, block)
    code_d_col = code_of(pc // n, rcd, block)
    code_a_ref[...] = code_a_row
    code_d_ref[...] = code_d_col
    respond(mob_ref, force_ref, vel, slots, width)
    pack_rows(code_a_row, vel[...], buf_ref)
    na = local_a(pr) + 1
    nd = pr % n + 1
    row16 = lax.broadcasted_iota(I32, (16, n), 0)
    va = jnp.where(row16 == 0, na // 256, jnp.where(row16 == 1, na % 256, 0)).astype(F32).astype(BF16)
    vd = jnp.where(row16 == 2, nd // 256, jnp.where(row16 == 3, nd % 256, 0)).astype(F32).astype(BF16)
    most = jnp.maximum(most_a, most_d)
    over = jnp.where(most > cap, 1.0, 0.0)

    def body(i):
        j = lax.broadcasted_iota(I32, (n, LANES), 1) + i * LANES
        aux = dot(va, onehot(j == code_a_col)) + dot(vd, onehot(j == code_d_col))
        aux_ref[i] = aux

    each(groups * block // LANES, body)
    parts = block // LANES
    rest = jnp.full((aux_rows(block) - 4 * parts, LANES), over, F32)
    for d in range(groups):
        rows = [aux_ref[d * parts + k][0:4] for k in range(parts)] + [rest]
        buf_ref[d * block + cap:(d + 1) * block, :] = jnp.concatenate(rows, 0).astype(BF16)
    hold.wait()


def index_kernel(groups, block, buf_ref, na_ref, nd_ref, over_ref):
    over = jnp.zeros((1, LANES), F32)
    parts = block // LANES
    for d in range(groups):
        aux = buf_ref[d * block + capacity(block):(d + 1) * block, :].astype(F32)
        for k in range(parts):
            lanes = slice(d * block + k * LANES, d * block + (k + 1) * LANES)
            a = aux[4 * k:4 * k + 4]
            na_ref[:, lanes] = (a[0:1] * 256 + a[1:2]).astype(I32) - 1
            nd_ref[:, lanes] = (a[2:3] * 256 + a[3:4]).astype(I32) - 1
        over = jnp.maximum(over, aux[4 * parts:4 * parts + 1])
    over_ref[...] = over.astype(I32)


def unpack_kernel(na_ref, buf_ref, out_ref, total):
    copies, n, _ = out_ref.shape
    step = 256
    total[...] = jnp.zeros(total.shape, F32)

    def body(i):
        pick = onehot(lax.broadcasted_iota(I32, (n, step), 0) == na_ref[:, at(i * step, step)])
        total[...] += dot(pick, buf_ref[at(i * step, step), :])

    each(buf_ref.shape[0] // step, body)
    natural = total[...].astype(BF16)
    for k in range(copies):
        out_ref[k] = natural


def product_kernel(first, half_ref, z_ref, g_ref, acc_ref, out_ref, f_ref, t_ref):
    tiles, blocks, rows, lanes = g_ref.shape
    depth = tiles * rows
    columns = pl.ds(pl.multiple_of(half_ref[0] * depth, LANES), depth)
    for i in range(blocks // 2):
        for t in range(tiles):
            at_rows = slice(t * rows, (t + 1) * rows)
            for b in range(2):
                at_lanes = slice(b * lanes, (b + 1) * lanes)
                x = g_ref[t, 2 * i + b]
                f_ref[i, at_rows, at_lanes] = x
                t_ref[i, at_rows, at_lanes] = turned(x.astype(F32)).astype(BF16)
        r = dot(z_ref[0, :, columns], f_ref[i]) + dot(z_ref[1, :, columns], t_ref[i])
        if first:
            out_ref[i] = r
        else:
            r = (acc_ref[i] + r).astype(BF16)
            out_ref[2 * i] = r[:, :lanes]
            out_ref[2 * i + 1] = r[:, lanes:]


def first_product_kernel(half_ref, z_ref, g_ref, out_ref, f_ref, t_ref):
    product_kernel(True, half_ref, z_ref, g_ref, None, out_ref, f_ref, t_ref)


def second_product_kernel(half_ref, z_ref, g_ref, acc_ref, out_ref, f_ref, t_ref):
    product_kernel(False, half_ref, z_ref, g_ref, acc_ref, out_ref, f_ref, t_ref)


def pressure_kernel(part_ref, ndc_ref, p_ref, buf_ref):
    total = part_ref[0].astype(F32)
    for b in range(1, part_ref.shape[0]):
        total += part_ref[b].astype(F32)
    p_ref[...] = total.astype(BF16)
    n = p_ref.shape[0]
    step = 256

    def body(i):
        pick = onehot(lax.broadcasted_iota(I32, (step, n), 1) == ndc_ref[at(i * step, step), :])
        buf_ref[at(i * step, step), :] = dot(pick, p_ref[...]).astype(BF16)

    each(buf_ref.shape[0] // step, body)


def response_kernel(slots, width, pack, buf_ref, force_ref, mob_ref, code_d_ref, code_a_ref, out_ref, drive, vel, total):
    n = force_ref.shape[0]
    step = 256
    total[...] = jnp.zeros(total.shape, F32)

    def body(i):
        j = lax.broadcasted_iota(I32, (n, step), 1) + i * step
        total[...] += dot(onehot(j == code_d_ref[...]), buf_ref[at(i * step, step), :])

    each(buf_ref.shape[0] // step, body)
    drive[...] = (force_ref[...].astype(F32) - total[...]).astype(BF16)
    if pack:
        respond(mob_ref, drive, vel, slots, width)
        pack_rows(code_a_ref[...], vel[...], out_ref)
    else:
        respond(mob_ref, drive, vel, slots, width)
        from_rows(vel, out_ref, total, slots, width)


def sds(*shape, dtype=BF16):
    return jax.ShapeDtypeStruct(shape, dtype)


def product_call(kernel, half, impedance, field, acc):
    _, n, depth = impedance.shape
    depth //= 2
    tiles, blocks, rows, lanes = field.shape
    first = acc is None
    return pl.pallas_call(
        kernel,
        out_shape=sds(blocks // 2, n, 2 * lanes, dtype=F32) if first else sds(blocks, n, lanes),
        in_specs=[pl.BlockSpec(memory_space=pltpu.SMEM)] + vmem(2 if first else 3),
        out_specs=vmem(1)[0],
        scratch_shapes=[pltpu.VMEM((blocks // 2, depth, 2 * lanes), BF16)] * 2,
        compiler_params=params(32),
        cost_estimate=pl.CostEstimate(flops=4 * n * depth * blocks * lanes, bytes_accessed=10 * 1024 * 1024, transcendentals=0),
        name="product",
    )(half, impedance, field, *([] if first else [acc]))


def per_device(impedance, mobility, force, patch_map, ownership):
    slots, width, _ = mobility.shape
    loads = force.shape[0]
    tile = ("chip", "core")
    chips = lax.axis_size("chip")
    groups = chips * 2
    col_tiles = lax.axis_size("col")
    n = slots * width
    lanes = 2 * loads
    patches = patch_map.reshape(-1, width)[ownership].reshape(n)
    force_rows = force.reshape(loads * slots, 2 * width)
    core = lax.axis_index("core").astype(I32)

    def exchange(buf):
        return lax.all_to_all(buf.reshape(groups, -1, lanes), tile, 0, 0).reshape(buf.shape)

    def begin(block):
        rows = groups * block
        buf, code_a, code_d, force_t, held = pl.pallas_call(
            functools.partial(start_kernel, groups, col_tiles, slots, width, block),
            out_shape=(sds(rows, lanes), sds(1, n, dtype=I32), sds(n, 1, dtype=I32), sds(n, lanes), pltpu.VMEM(impedance.shape, BF16)),
            in_specs=vmem(4) + [pl.BlockSpec(memory_space=pl.ANY)],
            out_specs=tuple(vmem(5)),
            scratch_shapes=[
                pltpu.VMEM((n, lanes), BF16),
                pltpu.VMEM((rows // LANES, 16, LANES), F32),
                pltpu.VMEM((loads * slots, 2 * width), F32),
                pltpu.SemaphoreType.DMA,
            ],
            compiler_params=params(48),
            name="start",
        )(patches[:, None], patches[None, :], force_rows, mobility, impedance)
        buf = exchange(buf)
        na, nd, over = pl.pallas_call(
            functools.partial(index_kernel, groups, block),
            out_shape=(sds(1, rows, dtype=I32), sds(1, rows, dtype=I32), sds(1, LANES, dtype=I32)),
            in_specs=vmem(1),
            out_specs=tuple(vmem(3)),
            compiler_params=params(32),
            name="positions",
        )(buf)
        return (buf, held, force_t, code_a, code_d, na, nd), over

    def iterate(received, held, force_t, code_a, code_d, na, nd):
        rows = received.shape[0]
        nd_col = nd.reshape(rows, 1)
        for iteration in range(ITERS):
            natural = pl.pallas_call(
                unpack_kernel,
                out_shape=sds(chips, n, lanes),
                in_specs=vmem(2),
                out_specs=vmem(1)[0],
                scratch_shapes=[pltpu.VMEM((n, lanes), F32)],
                compiler_params=params(40),
                name="unpack",
            )(na, received)
            pieces = natural.reshape(chips * col_tiles, n // col_tiles, lanes)
            mine = lax.all_to_all(pieces, ("chip", "col"), 0, 0)
            other = lax.ppermute(mine, "core", [(0, 1), (1, 0)])
            shape = (chips, col_tiles, n // col_tiles, lanes)
            acc = product_call(first_product_kernel, core[None], held, mine.reshape(shape), None)
            part = product_call(second_product_kernel, 1 - core[None], held, other.reshape(shape), acc)
            part = lax.all_to_all(part, "col", 0, 0)
            pressure, out = pl.pallas_call(
                pressure_kernel,
                out_shape=(sds(n, lanes), sds(rows, lanes)),
                in_specs=vmem(2),
                out_specs=tuple(vmem(2)),
                compiler_params=params(48),
                name="pressure",
            )(part, nd_col)
            back = exchange(out)
            pack = iteration < ITERS - 1
            velocity = pl.pallas_call(
                functools.partial(response_kernel, slots, width, pack),
                out_shape=sds(rows if pack else n, lanes),
                in_specs=vmem(5),
                out_specs=vmem(1)[0],
                scratch_shapes=[pltpu.VMEM((n, lanes), BF16), pltpu.VMEM((n, lanes), BF16), pltpu.VMEM((n, lanes), F32)],
                compiler_params=params(48),
                name="response",
            )(back, force_t, mobility, code_d, code_a)
            if pack:
                received = exchange(velocity)
        return velocity, pressure

    begun, over = begin(USUAL)
    usual = iterate(*begun)

    def any_permutation():
        return iterate(*begin(LARGEST)[0])

    velocity, pressure = lax.cond(over[0, 0] == 0, lambda: usual, any_permutation)
    velocity = velocity.reshape(loads, slots, 2 * width)
    pressure = pressure.reshape(n, 2, loads).transpose(2, 1, 0)
    return velocity, pressure


def solution(mesh):
    tiles, cols = mesh.devices.shape
    cores = Mesh(mesh.devices.reshape(tiles // 2, 2, cols), ("chip", "core", "col"))
    tile = ("chip", "core")
    return jax.shard_map(
        per_device,
        mesh=cores,
        in_specs=(
            P(None, tile, "col"),
            P(tile, None, None),
            P("col", tile, None),
            P(),
            P(tile),
        ),
        out_specs=(P("col", tile, None), P("col", None, tile)),
        check_vma=False,
    )
```

```python
import functools

import jax
import jax.numpy as jnp
from jax import lax
from jax.experimental import pallas as pl
from jax.experimental.pallas import tpu as pltpu
from jax.sharding import Mesh
from jax.sharding import PartitionSpec as P

ITERS = 2
LANES = 128
USUAL = 128
LARGEST = 1152
BF16 = jnp.bfloat16
F32 = jnp.float32
I32 = jnp.int32


def vmem(n):
    return [pl.BlockSpec(memory_space=pltpu.VMEM)] * n


def params(rows):
    return pltpu.CompilerParams(vmem_limit_bytes=(20 if rows <= 4096 else 48) * 1024 * 1024)


def dot(a, b):
    return jnp.dot(a, b, preferred_element_type=F32)


def onehot(cond):
    return jnp.where(cond, 1.0, 0.0).astype(BF16)


def turned(x):
    half = x.shape[-1] // 2
    rolled = pltpu.roll(x, half, x.ndim - 1)
    lane = lax.broadcasted_iota(I32, x.shape, x.ndim - 1)
    return jnp.where(lane < half, -rolled, rolled)


def respond(mob_ref, drive_ref, out_ref, slots, width):
    for s in range(slots):
        d = drive_ref[s * width:(s + 1) * width, :]
        t = turned(d.astype(F32)).astype(BF16)
        both = jnp.concatenate([d, t], 0)
        out_ref[s * width:(s + 1) * width, :] = dot(mob_ref[s], both).astype(BF16)


def column_of(row):
    n = row.shape[1]
    wide = [jnp.broadcast_to(row[:, i:i + LANES].astype(F32), (LANES, LANES)).T for i in range(0, n, LANES)]
    return jnp.concatenate(wide, 0)[:, :1].astype(row.dtype)


def ranks(dest_a, dest_d, groups):
    n = dest_a.shape[1]
    group = lax.broadcasted_iota(I32, (2 * groups, LANES), 0)
    before = onehot(lax.broadcasted_iota(I32, (LANES, LANES), 0) < lax.broadcasted_iota(I32, (LANES, LANES), 1))
    count = jnp.zeros((2 * groups, 1), F32)
    rank_a, rank_d = [], []
    for i in range(0, n, LANES):
        is_a = group == dest_a[:, i:i + LANES]
        is_d = group == dest_d[:, i:i + LANES] + groups
        one = jnp.where(is_a | is_d, 1.0, 0.0)
        place = dot(one.astype(BF16), before) + count
        rank_a.append(jnp.sum(jnp.where(is_a, place, 0.0), 0, keepdims=True))
        rank_d.append(jnp.sum(jnp.where(is_d, place, 0.0), 0, keepdims=True))
        count += jnp.sum(one, 1, keepdims=True)
    return jnp.concatenate(rank_a, 1).astype(I32), jnp.concatenate(rank_d, 1).astype(I32), jnp.max(count)


def own_patches(own_ref, map_ref, out_ref, slots, width):
    lane = lax.broadcasted_iota(I32, (1, LANES), 1)
    per = LANES // width
    for s in range(0, slots, per):
        row = jnp.zeros((1, LANES), I32)
        for k in range(per):
            panel = own_ref[s + k]
            found = map_ref[pl.ds(panel // per, 1), :]
            for shift in range(per):
                moved = pltpu.roll(found, ((k - shift) % per) * width, 1)
                here = (lane // width == k) & (panel % per == shift)
                row = jnp.where(here, moved, row)
        out_ref[:, s * width:s * width + LANES] = row


def aux_rows(block):
    return -(-(4 * block // LANES + 1) // 16) * 16


def capacity(block):
    return block - aux_rows(block)


def each(count, body):
    if count <= 16:
        for i in range(count):
            body(i)
    else:
        pl.loop(0, count)(body)


def at(start, size):
    if isinstance(start, int):
        return slice(start, start + size)
    return pl.ds(pl.multiple_of(start, 128), size)


def code_of(dest, rank, block, cap):
    return jnp.where(rank < cap, dest * block + rank, -1)


def pack_rows(code_row, rows, out_ref):
    n = rows.shape[0]
    step = 256

    def body(i):
        j = lax.broadcasted_iota(I32, (step, n), 0) + i * step
        out_ref[at(i * step, step), :] = dot(onehot(j == code_row), rows).astype(BF16)

    each(out_ref.shape[0] // step, body)


def to_rows(in_ref, out_ref, stage, slots, width):
    stage[...] = in_ref[...].astype(F32)
    loads = in_ref.shape[0] // slots
    for s in range(slots):
        x = stage[pl.ds(s, loads, stride=slots), :].T
        out_ref[s * width:(s + 1) * width, :] = jnp.concatenate([x[:width], x[width:]], 1).astype(BF16)


def from_rows(rows, out_ref, stage, slots, width):
    loads = out_ref.shape[0] // slots
    for s in range(slots):
        x = rows[s * width:(s + 1) * width, :].astype(F32)
        x = jnp.concatenate([x[:, :loads], x[:, loads:]], 0).T
        stage[pl.ds(s, loads, stride=slots), :] = x
    out_ref[...] = stage[...].astype(BF16)


def start_kernel(
    groups, col_tiles, slots, width, block, own_ref, map_ref, loads_ref, mob_ref,
    buf_ref, code_a_ref, code_d_ref, force_ref, vel, aux_ref, stage, patch_ref,
):
    to_rows(loads_ref, force_ref, stage, slots, width)
    own_patches(own_ref, map_ref, patch_ref, slots, width)
    pr = patch_ref[...]
    n = pr.shape[1]
    col_width = n * groups // col_tiles
    chunk = n // col_tiles
    cap = capacity(block)
    q = (pr % col_width) // chunk
    dest_a = (q % (groups // 2)) * 2 + q // (groups // 2)
    local_a = (pr // col_width) * chunk + pr % chunk
    dest_d = pr // n
    rank_a, rank_d, most = ranks(dest_a, dest_d, groups)
    code_a_row = code_of(dest_a, rank_a, block, cap)
    code_a_col = column_of(code_a_row)
    code_d_col = column_of(code_of(dest_d, rank_d, block, cap))
    code_a_ref[...] = code_of(dest_a, rank_a, cap, cap)
    code_d_ref[...] = column_of(code_of(dest_d, rank_d, cap, cap))
    respond(mob_ref, force_ref, vel, slots, width)
    pack_rows(code_a_row, vel[...], buf_ref)
    na = local_a + 1
    nd = pr % n + 1
    row16 = lax.broadcasted_iota(I32, (16, n), 0)
    va = jnp.where(row16 == 0, na // 256, jnp.where(row16 == 1, na % 256, 0)).astype(F32).astype(BF16)
    vd = jnp.where(row16 == 2, nd // 256, jnp.where(row16 == 3, nd % 256, 0)).astype(F32).astype(BF16)
    over = jnp.where(most > cap, 1.0, 0.0)

    def body(i):
        j = lax.broadcasted_iota(I32, (n, LANES), 1) + i * LANES
        aux = dot(va, onehot(j == code_a_col)) + dot(vd, onehot(j == code_d_col))
        aux_ref[i] = aux

    each(groups * block // LANES, body)
    parts = block // LANES
    rest = jnp.full((aux_rows(block) - 4 * parts, LANES), over, F32)
    for d in range(groups):
        rows = [aux_ref[d * parts + k][0:4] for k in range(parts)] + [rest]
        buf_ref[d * block + cap:(d + 1) * block, :] = jnp.concatenate(rows, 0).astype(BF16)


def index_kernel(groups, block, buf_ref, data_ref, na_ref, ndc_ref, over_ref):
    over = jnp.zeros((1, LANES), F32)
    cap = capacity(block)
    parts = block // LANES
    for d in range(groups):
        data_ref[d * cap:(d + 1) * cap, :] = buf_ref[d * block:d * block + cap, :]
        aux = buf_ref[d * block + cap:(d + 1) * block, :].astype(F32)
        for k in range(0, cap, LANES):
            size = min(LANES, cap - k)
            a = aux[k // LANES * 4:k // LANES * 4 + 4]
            to = d * cap + k
            na_ref[:, to:to + size] = ((a[0:1] * 256 + a[1:2]).astype(I32) - 1)[:, :size]
            ndc_ref[to:to + size, :] = column_of((a[2:3] * 256 + a[3:4]).astype(I32) - 1)[:size]
        over = jnp.maximum(over, aux[4 * parts:4 * parts + 1])
    over_ref[...] = over.astype(I32)


def unpack_kernel(na_ref, buf_ref, out_ref, total):
    copies, n, _ = out_ref.shape
    step = 256
    total[...] = jnp.zeros(total.shape, F32)

    def body(i):
        pick = onehot(lax.broadcasted_iota(I32, (n, step), 0) == na_ref[:, at(i * step, step)])
        total[...] += dot(pick, buf_ref[at(i * step, step), :])

    each(buf_ref.shape[0] // step, body)
    natural = total[...].astype(BF16)
    for k in range(copies):
        out_ref[k] = natural


def product_kernel(first, half_ref, z_ref, g_ref, acc_ref, out_ref, f_ref, t_ref, z_part, sems):
    tiles, blocks, rows, lanes = g_ref.shape
    depth = tiles * rows
    steps = sems.shape[0]
    height = z_ref.shape[1] // steps
    columns = pl.ds(pl.multiple_of(half_ref[0] * depth, LANES), depth)
    loads = []
    for r in range(steps):
        at_rows = slice(r * height, (r + 1) * height)
        loads.append(pltpu.make_async_copy(z_ref.at[:, at_rows, columns], z_part.at[r], sems.at[r]))
        loads[r].start()

    def fill(i):
        for t in range(tiles):
            at_rows = slice(t * rows, (t + 1) * rows)
            for b in range(2):
                at_lanes = slice(b * lanes, (b + 1) * lanes)
                x = g_ref[t, 2 * i + b]
                f_ref[i, at_rows, at_lanes] = x
                t_ref[i, at_rows, at_lanes] = turned(x.astype(F32)).astype(BF16)

    for r in range(steps):
        out_rows = slice(r * height, (r + 1) * height)
        for i in range(blocks // 2):
            if r == 0 and i == 0:
                fill(0)
                fill(1)
            if i == 0:
                loads[r].wait()
            if r == 0 and 0 < i < blocks // 2 - 1:
                fill(i + 1)
            p = dot(z_part[r, 0], f_ref[i]) + dot(z_part[r, 1], t_ref[i])
            if first:
                out_ref[i, out_rows, :] = p
            else:
                p = (acc_ref[i, out_rows, :] + p).astype(BF16)
                out_ref[2 * i, out_rows, :] = p[:, :lanes]
                out_ref[2 * i + 1, out_rows, :] = p[:, lanes:]


def first_product_kernel(half_ref, z_ref, g_ref, out_ref, *scratch):
    product_kernel(True, half_ref, z_ref, g_ref, None, out_ref, *scratch)


def second_product_kernel(half_ref, z_ref, g_ref, acc_ref, out_ref, *scratch):
    product_kernel(False, half_ref, z_ref, g_ref, acc_ref, out_ref, *scratch)


def pressure_kernel(part_ref, ndc_ref, p_ref, buf_ref):
    total = part_ref[0].astype(F32)
    for b in range(1, part_ref.shape[0]):
        total += part_ref[b].astype(F32)
    p_ref[...] = total.astype(BF16)
    n = p_ref.shape[0]
    step = 256

    def body(i):
        pick = onehot(lax.broadcasted_iota(I32, (step, n), 1) == ndc_ref[at(i * step, step), :])
        buf_ref[at(i * step, step), :] = dot(pick, p_ref[...]).astype(BF16)

    each(buf_ref.shape[0] // step, body)


def response_kernel(slots, width, pack, buf_ref, force_ref, mob_ref, code_d_ref, code_a_ref, out_ref, drive, vel, total):
    n = force_ref.shape[0]
    step = 256
    total[...] = jnp.zeros(total.shape, F32)

    def body(i):
        j = lax.broadcasted_iota(I32, (n, step), 1) + i * step
        total[...] += dot(onehot(j == code_d_ref[...]), buf_ref[at(i * step, step), :])

    each(buf_ref.shape[0] // step, body)
    drive[...] = (force_ref[...].astype(F32) - total[...]).astype(BF16)
    if pack:
        respond(mob_ref, drive, vel, slots, width)
        pack_rows(code_a_ref[...], vel[...], out_ref)
    else:
        respond(mob_ref, drive, vel, slots, width)
        from_rows(vel, out_ref, total, slots, width)


def sds(*shape, dtype=BF16):
    return jax.ShapeDtypeStruct(shape, dtype)


def product_call(kernel, half, impedance, field, acc):
    _, n, depth = impedance.shape
    depth //= 2
    tiles, blocks, rows, lanes = field.shape
    first = acc is None
    steps = 4
    return pl.pallas_call(
        kernel,
        out_shape=sds(blocks // 2, n, 2 * lanes, dtype=F32) if first else sds(blocks, n, lanes),
        in_specs=[
            pl.BlockSpec(memory_space=pltpu.SMEM),
            pl.BlockSpec(memory_space=pl.ANY),
        ] + vmem(1 if first else 2),
        out_specs=vmem(1)[0],
        scratch_shapes=[
            pltpu.VMEM((blocks // 2, depth, 2 * lanes), BF16),
            pltpu.VMEM((blocks // 2, depth, 2 * lanes), BF16),
            pltpu.VMEM((steps, 2, n // steps, depth), BF16),
            pltpu.SemaphoreType.DMA((steps,)),
        ],
        compiler_params=params(0),
        cost_estimate=pl.CostEstimate(flops=4 * n * depth * blocks * lanes, bytes_accessed=10 * 1024 * 1024, transcendentals=0),
        name="product",
    )(half, impedance, field, *([] if first else [acc]))


def per_device(impedance, mobility, force, patch_map, ownership):
    slots, width, _ = mobility.shape
    loads = force.shape[0]
    tile = ("chip", "core")
    chips = lax.axis_size("chip")
    groups = chips * 2
    col_tiles = lax.axis_size("col")
    n = slots * width
    lanes = 2 * loads
    force_rows = force.reshape(loads * slots, 2 * width)
    core = lax.axis_index("core").astype(I32)

    def exchange(buf):
        return lax.all_to_all(buf.reshape(groups, -1, lanes), tile, 0, 0).reshape(buf.shape)

    def begin(block):
        rows = groups * block
        buf, code_a, code_d, force_t = pl.pallas_call(
            functools.partial(start_kernel, groups, col_tiles, slots, width, block),
            out_shape=(sds(rows, lanes), sds(1, n, dtype=I32), sds(n, 1, dtype=I32), sds(n, lanes)),
            in_specs=[pl.BlockSpec(memory_space=pltpu.SMEM)] + vmem(3),
            out_specs=tuple(vmem(4)),
            scratch_shapes=[
                pltpu.VMEM((n, lanes), BF16),
                pltpu.VMEM((rows // LANES, 16, LANES), F32),
                pltpu.VMEM((loads * slots, 2 * width), F32),
                pltpu.VMEM((1, n), I32),
            ],
            compiler_params=params(rows),
            name="start",
        )(ownership, patch_map.reshape(-1, LANES), force_rows, mobility)
        buf = exchange(buf)
        kept = groups * capacity(block)
        data, na, nd_col, over = pl.pallas_call(
            functools.partial(index_kernel, groups, block),
            out_shape=(sds(kept, lanes), sds(1, kept, dtype=I32), sds(kept, 1, dtype=I32), sds(1, LANES, dtype=I32)),
            in_specs=vmem(1),
            out_specs=tuple(vmem(4)),
            compiler_params=params(rows),
            name="positions",
        )(buf)
        return (data, force_t, code_a, code_d, na, nd_col), over

    def iterate(received, force_t, code_a, code_d, na, nd_col):
        rows = received.shape[0]
        for iteration in range(ITERS):
            natural = pl.pallas_call(
                unpack_kernel,
                out_shape=sds(chips, n, lanes),
                in_specs=vmem(2),
                out_specs=vmem(1)[0],
                scratch_shapes=[pltpu.VMEM((n, lanes), F32)],
                compiler_params=params(rows),
                name="unpack",
            )(na, received)
            pieces = natural.reshape(chips * col_tiles, n // col_tiles, lanes)
            mine = lax.all_to_all(pieces, ("chip", "col"), 0, 0)
            other = lax.ppermute(mine, "core", [(0, 1), (1, 0)])
            shape = (chips, col_tiles, n // col_tiles, lanes)
            acc = product_call(first_product_kernel, core[None], impedance, mine.reshape(shape), None)
            part = product_call(second_product_kernel, 1 - core[None], impedance, other.reshape(shape), acc)
            part = lax.all_to_all(part, "col", 0, 0)
            pressure, out = pl.pallas_call(
                pressure_kernel,
                out_shape=(sds(n, lanes), sds(rows, lanes)),
                in_specs=vmem(2),
                out_specs=tuple(vmem(2)),
                compiler_params=params(rows),
                name="pressure",
            )(part, nd_col)
            back = exchange(out)
            pack = iteration < ITERS - 1
            velocity = pl.pallas_call(
                functools.partial(response_kernel, slots, width, pack),
                out_shape=sds(rows if pack else n, lanes),
                in_specs=vmem(5),
                out_specs=vmem(1)[0],
                scratch_shapes=[pltpu.VMEM((n, lanes), BF16), pltpu.VMEM((n, lanes), BF16), pltpu.VMEM((n, lanes), F32)],
                compiler_params=params(rows),
                name="response",
            )(back, force_t, mobility, code_d, code_a)
            if pack:
                received = exchange(velocity)
        return velocity, pressure

    begun, over = begin(USUAL)
    usual = iterate(*begun)

    def any_permutation():
        return iterate(*begin(LARGEST)[0])

    velocity, pressure = lax.cond(over[0, 0] == 0, lambda: usual, any_permutation)
    velocity = velocity.reshape(loads, slots, 2 * width)
    pressure = pressure.reshape(n, 2, loads).transpose(2, 1, 0)
    return velocity, pressure


def solution(mesh):
    tiles, cols = mesh.devices.shape
    cores = Mesh(mesh.devices.reshape(tiles // 2, 2, cols), ("chip", "core", "col"))
    tile = ("chip", "core")
    return jax.shard_map(
        per_device,
        mesh=cores,
        in_specs=(
            P(None, tile, "col"),
            P(tile, None, None),
            P("col", tile, None),
            P(),
            P(tile),
        ),
        out_specs=(P("col", tile, None), P("col", None, tile)),
        check_vma=False,
    )
```

```python
import functools

import jax
import jax.numpy as jnp
from jax import lax
from jax.experimental import pallas as pl
from jax.experimental.pallas import tpu as pltpu
from jax.sharding import Mesh
from jax.sharding import PartitionSpec as P

ITERS = 2
LANES = 128
USUAL = 128
LARGEST = 1152
BF16 = jnp.bfloat16
F32 = jnp.float32
I32 = jnp.int32


def vmem(n):
    return [pl.BlockSpec(memory_space=pltpu.VMEM)] * n


def params(rows):
    return pltpu.CompilerParams(vmem_limit_bytes=(20 if rows <= 4096 else 48) * 1024 * 1024)


def dot(a, b):
    return jnp.dot(a, b, preferred_element_type=F32)


def onehot(cond):
    return jnp.where(cond, 1.0, 0.0).astype(BF16)


def turned(x):
    half = x.shape[-1] // 2
    rolled = pltpu.roll(x, half, x.ndim - 1)
    lane = lax.broadcasted_iota(I32, x.shape, x.ndim - 1)
    return jnp.where(lane < half, -rolled, rolled)


def respond(mob_ref, drive_ref, out_ref, slots, width):
    for s in range(slots):
        d = drive_ref[s * width:(s + 1) * width, :]
        t = turned(d.astype(F32)).astype(BF16)
        both = jnp.concatenate([d, t], 0)
        out_ref[s * width:(s + 1) * width, :] = dot(mob_ref[s], both).astype(BF16)


def column_of(row):
    n = row.shape[1]
    wide = [jnp.broadcast_to(row[:, i:i + LANES].astype(F32), (LANES, LANES)).T for i in range(0, n, LANES)]
    return jnp.concatenate(wide, 0)[:, :1].astype(row.dtype)


def ranks(dest_a, dest_d, groups):
    n = dest_a.shape[1]
    group = lax.broadcasted_iota(I32, (2 * groups, LANES), 0)
    before = onehot(lax.broadcasted_iota(I32, (LANES, LANES), 0) < lax.broadcasted_iota(I32, (LANES, LANES), 1))
    count = jnp.zeros((2 * groups, 1), F32)
    rank_a, rank_d = [], []
    for i in range(0, n, LANES):
        is_a = group == dest_a[:, i:i + LANES]
        is_d = group == dest_d[:, i:i + LANES] + groups
        one = jnp.where(is_a | is_d, 1.0, 0.0)
        place = dot(one.astype(BF16), before) + count
        rank_a.append(jnp.sum(jnp.where(is_a, place, 0.0), 0, keepdims=True))
        rank_d.append(jnp.sum(jnp.where(is_d, place, 0.0), 0, keepdims=True))
        count += jnp.sum(one, 1, keepdims=True)
    return jnp.concatenate(rank_a, 1).astype(I32), jnp.concatenate(rank_d, 1).astype(I32), jnp.max(count)


def own_patches(own_ref, map_ref, out_ref, slots, width):
    lane = lax.broadcasted_iota(I32, (1, LANES), 1)
    per = LANES // width
    for s in range(0, slots, per):
        row = jnp.zeros((1, LANES), I32)
        for k in range(per):
            panel = own_ref[s + k]
            found = map_ref[pl.ds(panel // per, 1), :]
            for shift in range(per):
                moved = pltpu.roll(found, ((k - shift) % per) * width, 1)
                here = (lane // width == k) & (panel % per == shift)
                row = jnp.where(here, moved, row)
        out_ref[:, s * width:s * width + LANES] = row


def aux_rows(block):
    return -(-(4 * block // LANES + 1) // 16) * 16


def capacity(block):
    return block - aux_rows(block)


def each(count, body):
    if count <= 16:
        for i in range(count):
            body(i)
    else:
        pl.loop(0, count)(body)


def at(start, size):
    if isinstance(start, int):
        return slice(start, start + size)
    return pl.ds(pl.multiple_of(start, 128), size)


def code_of(dest, rank, block, cap):
    return jnp.where(rank < cap, dest * block + rank, -1)


def pack_rows(code_row, rows, out_ref):
    n = rows.shape[0]
    step = 256

    def body(i):
        j = lax.broadcasted_iota(I32, (step, n), 0) + i * step
        out_ref[at(i * step, step), :] = dot(onehot(j == code_row), rows).astype(BF16)

    each(out_ref.shape[0] // step, body)


def to_rows(in_ref, out_ref, stage, slots, width):
    stage[...] = in_ref[...].astype(F32)
    loads = in_ref.shape[0] // slots
    for s in range(slots):
        x = stage[pl.ds(s, loads, stride=slots), :].T
        out_ref[s * width:(s + 1) * width, :] = jnp.concatenate([x[:width], x[width:]], 1).astype(BF16)


def from_rows(rows, out_ref, stage, slots, width):
    loads = out_ref.shape[0] // slots
    for s in range(slots):
        x = rows[s * width:(s + 1) * width, :].astype(F32)
        x = jnp.concatenate([x[:, :loads], x[:, loads:]], 0).T
        stage[pl.ds(s, loads, stride=slots), :] = x
    out_ref[...] = stage[...].astype(BF16)


def start_kernel(
    groups, col_tiles, slots, width, block, own_ref, map_ref, loads_ref, mob_ref,
    buf_ref, code_a_ref, code_d_ref, force_ref, vel, aux_ref, stage, patch_ref,
):
    to_rows(loads_ref, force_ref, stage, slots, width)
    own_patches(own_ref, map_ref, patch_ref, slots, width)
    pr = patch_ref[...]
    n = pr.shape[1]
    col_width = n * groups // col_tiles
    chunk = n // col_tiles
    cap = capacity(block)
    q = (pr % col_width) // chunk
    dest_a = (q % (groups // 2)) * 2 + q // (groups // 2)
    local_a = (pr // col_width) * chunk + pr % chunk
    dest_d = pr // n
    rank_a, rank_d, most = ranks(dest_a, dest_d, groups)
    code_a_row = code_of(dest_a, rank_a, block, cap)
    code_a_col = column_of(code_a_row)
    code_d_col = column_of(code_of(dest_d, rank_d, block, cap))
    code_a_ref[...] = code_of(dest_a, rank_a, cap, cap)
    code_d_ref[...] = column_of(code_of(dest_d, rank_d, cap, cap))
    respond(mob_ref, force_ref, vel, slots, width)
    pack_rows(code_a_row, vel[...], buf_ref)
    na = local_a + 1
    nd = pr % n + 1
    row16 = lax.broadcasted_iota(I32, (16, n), 0)
    va = jnp.where(row16 == 0, na // 256, jnp.where(row16 == 1, na % 256, 0)).astype(F32).astype(BF16)
    vd = jnp.where(row16 == 2, nd // 256, jnp.where(row16 == 3, nd % 256, 0)).astype(F32).astype(BF16)
    over = jnp.where(most > cap, 1.0, 0.0)

    def body(i):
        j = lax.broadcasted_iota(I32, (n, LANES), 1) + i * LANES
        aux = dot(va, onehot(j == code_a_col)) + dot(vd, onehot(j == code_d_col))
        aux_ref[i] = aux

    each(groups * block // LANES, body)
    parts = block // LANES
    rest = jnp.full((aux_rows(block) - 4 * parts, LANES), over, F32)
    for d in range(groups):
        rows = [aux_ref[d * parts + k][0:4] for k in range(parts)] + [rest]
        buf_ref[d * block + cap:(d + 1) * block, :] = jnp.concatenate(rows, 0).astype(BF16)


def index_kernel(groups, block, buf_ref, data_ref, na_ref, ndc_ref, over_ref):
    over = jnp.zeros((1, LANES), F32)
    cap = capacity(block)
    parts = block // LANES
    for d in range(groups):
        data_ref[d * cap:(d + 1) * cap, :] = buf_ref[d * block:d * block + cap, :]
        aux = buf_ref[d * block + cap:(d + 1) * block, :].astype(F32)
        for k in range(0, cap, LANES):
            size = min(LANES, cap - k)
            a = aux[k // LANES * 4:k // LANES * 4 + 4]
            to = d * cap + k
            na_ref[:, to:to + size] = ((a[0:1] * 256 + a[1:2]).astype(I32) - 1)[:, :size]
            ndc_ref[to:to + size, :] = column_of((a[2:3] * 256 + a[3:4]).astype(I32) - 1)[:size]
        over = jnp.maximum(over, aux[4 * parts:4 * parts + 1])
    over_ref[...] = over.astype(I32)


def unpack_kernel(na_ref, buf_ref, out_ref, total):
    copies, n, _ = out_ref.shape
    step = 256
    total[...] = jnp.zeros(total.shape, F32)

    def body(i):
        pick = onehot(lax.broadcasted_iota(I32, (n, step), 0) == na_ref[:, at(i * step, step)])
        total[...] += dot(pick, buf_ref[at(i * step, step), :])

    each(buf_ref.shape[0] // step, body)
    natural = total[...].astype(BF16)
    for k in range(copies):
        out_ref[k] = natural


def product_kernel(first, half_ref, z_ref, g_ref, acc_ref, out_ref, f_ref, t_ref, z_head, z_tail, sems):
    tiles, blocks, rows, lanes = g_ref.shape
    depth = tiles * rows
    head = z_head.shape[1]
    columns = pl.ds(pl.multiple_of(half_ref[0] * depth, LANES), depth)
    parts = [(z_head, slice(0, head)), (z_tail, slice(head, z_ref.shape[1]))]
    loads = []
    for r, (z_part, out_rows) in enumerate(parts):
        loads.append(pltpu.make_async_copy(z_ref.at[:, out_rows, columns], z_part, sems.at[r]))
        loads[r].start()

    def fill(i):
        for t in range(tiles):
            at_rows = slice(t * rows, (t + 1) * rows)
            for b in range(2):
                at_lanes = slice(b * lanes, (b + 1) * lanes)
                x = g_ref[t, 2 * i + b]
                f_ref[i, at_rows, at_lanes] = x
                t_ref[i, at_rows, at_lanes] = turned(x.astype(F32)).astype(BF16)

    for r, (z_part, out_rows) in enumerate(parts):
        for i in range(blocks // 2):
            if r == 0 and i == 0:
                fill(0)
                fill(1)
            if i == 0:
                loads[r].wait()
            if r == 0 and 0 < i < blocks // 2 - 1:
                fill(i + 1)
            p = dot(z_part[0], f_ref[i]) + dot(z_part[1], t_ref[i])
            if first:
                out_ref[i, out_rows, :] = p
            else:
                p = (acc_ref[i, out_rows, :] + p).astype(BF16)
                out_ref[2 * i, out_rows, :] = p[:, :lanes]
                out_ref[2 * i + 1, out_rows, :] = p[:, lanes:]


def first_product_kernel(half_ref, z_ref, g_ref, out_ref, *scratch):
    product_kernel(True, half_ref, z_ref, g_ref, None, out_ref, *scratch)


def second_product_kernel(half_ref, z_ref, g_ref, acc_ref, out_ref, *scratch):
    product_kernel(False, half_ref, z_ref, g_ref, acc_ref, out_ref, *scratch)


def pressure_kernel(part_ref, ndc_ref, p_ref, buf_ref):
    total = part_ref[0].astype(F32)
    for b in range(1, part_ref.shape[0]):
        total += part_ref[b].astype(F32)
    p_ref[...] = total.astype(BF16)
    n = p_ref.shape[0]
    step = 256

    def body(i):
        pick = onehot(lax.broadcasted_iota(I32, (step, n), 1) == ndc_ref[at(i * step, step), :])
        buf_ref[at(i * step, step), :] = dot(pick, p_ref[...]).astype(BF16)

    each(buf_ref.shape[0] // step, body)


def response_kernel(slots, width, pack, buf_ref, force_ref, mob_ref, code_d_ref, code_a_ref, out_ref, drive, vel, total):
    n = force_ref.shape[0]
    step = 256
    total[...] = jnp.zeros(total.shape, F32)

    def body(i):
        j = lax.broadcasted_iota(I32, (n, step), 1) + i * step
        total[...] += dot(onehot(j == code_d_ref[...]), buf_ref[at(i * step, step), :])

    each(buf_ref.shape[0] // step, body)
    drive[...] = (force_ref[...].astype(F32) - total[...]).astype(BF16)
    if pack:
        respond(mob_ref, drive, vel, slots, width)
        pack_rows(code_a_ref[...], vel[...], out_ref)
    else:
        respond(mob_ref, drive, vel, slots, width)
        from_rows(vel, out_ref, total, slots, width)


def sds(*shape, dtype=BF16):
    return jax.ShapeDtypeStruct(shape, dtype)


def product_call(kernel, half, impedance, field, acc):
    _, n, depth = impedance.shape
    depth //= 2
    tiles, blocks, rows, lanes = field.shape
    first = acc is None
    return pl.pallas_call(
        kernel,
        out_shape=sds(blocks // 2, n, 2 * lanes, dtype=F32) if first else sds(blocks, n, lanes),
        in_specs=[
            pl.BlockSpec(memory_space=pltpu.SMEM),
            pl.BlockSpec(memory_space=pl.ANY),
        ] + vmem(1 if first else 2),
        out_specs=vmem(1)[0],
        scratch_shapes=[
            pltpu.VMEM((blocks // 2, depth, 2 * lanes), BF16),
            pltpu.VMEM((blocks // 2, depth, 2 * lanes), BF16),
            pltpu.VMEM((2, n // 4, depth), BF16),
            pltpu.VMEM((2, n - n // 4, depth), BF16),
            pltpu.SemaphoreType.DMA((2,)),
        ],
        compiler_params=params(0),
        cost_estimate=pl.CostEstimate(flops=4 * n * depth * blocks * lanes, bytes_accessed=10 * 1024 * 1024, transcendentals=0),
        name="product",
    )(half, impedance, field, *([] if first else [acc]))


def per_device(impedance, mobility, force, patch_map, ownership):
    slots, width, _ = mobility.shape
    loads = force.shape[0]
    tile = ("chip", "core")
    chips = lax.axis_size("chip")
    groups = chips * 2
    col_tiles = lax.axis_size("col")
    n = slots * width
    lanes = 2 * loads
    force_rows = force.reshape(loads * slots, 2 * width)
    core = lax.axis_index("core").astype(I32)

    def exchange(buf):
        return lax.all_to_all(buf.reshape(groups, -1, lanes), tile, 0, 0).reshape(buf.shape)

    def begin(block):
        rows = groups * block
        buf, code_a, code_d, force_t = pl.pallas_call(
            functools.partial(start_kernel, groups, col_tiles, slots, width, block),
            out_shape=(sds(rows, lanes), sds(1, n, dtype=I32), sds(n, 1, dtype=I32), sds(n, lanes)),
            in_specs=[pl.BlockSpec(memory_space=pltpu.SMEM)] + vmem(3),
            out_specs=tuple(vmem(4)),
            scratch_shapes=[
                pltpu.VMEM((n, lanes), BF16),
                pltpu.VMEM((rows // LANES, 16, LANES), F32),
                pltpu.VMEM((loads * slots, 2 * width), F32),
                pltpu.VMEM((1, n), I32),
            ],
            compiler_params=params(rows),
            name="start",
        )(ownership, patch_map.reshape(-1, LANES), force_rows, mobility)
        buf = exchange(buf)
        kept = groups * capacity(block)
        data, na, nd_col, over = pl.pallas_call(
            functools.partial(index_kernel, groups, block),
            out_shape=(sds(kept, lanes), sds(1, kept, dtype=I32), sds(kept, 1, dtype=I32), sds(1, LANES, dtype=I32)),
            in_specs=vmem(1),
            out_specs=tuple(vmem(4)),
            compiler_params=params(rows),
            name="positions",
        )(buf)
        return (data, force_t, code_a, code_d, na, nd_col), over

    def iterate(received, force_t, code_a, code_d, na, nd_col):
        rows = received.shape[0]
        for iteration in range(ITERS):
            natural = pl.pallas_call(
                unpack_kernel,
                out_shape=sds(chips, n, lanes),
                in_specs=vmem(2),
                out_specs=vmem(1)[0],
                scratch_shapes=[pltpu.VMEM((n, lanes), F32)],
                compiler_params=params(rows),
                name="unpack",
            )(na, received)
            pieces = natural.reshape(chips * col_tiles, n // col_tiles, lanes)
            mine = lax.all_to_all(pieces, ("chip", "col"), 0, 0)
            other = lax.ppermute(mine, "core", [(0, 1), (1, 0)])
            shape = (chips, col_tiles, n // col_tiles, lanes)
            acc = product_call(first_product_kernel, core[None], impedance, mine.reshape(shape), None)
            part = product_call(second_product_kernel, 1 - core[None], impedance, other.reshape(shape), acc)
            part = lax.all_to_all(part, "col", 0, 0)
            pressure, out = pl.pallas_call(
                pressure_kernel,
                out_shape=(sds(n, lanes), sds(rows, lanes)),
                in_specs=vmem(2),
                out_specs=tuple(vmem(2)),
                compiler_params=params(rows),
                name="pressure",
            )(part, nd_col)
            back = exchange(out)
            pack = iteration < ITERS - 1
            velocity = pl.pallas_call(
                functools.partial(response_kernel, slots, width, pack),
                out_shape=sds(rows if pack else n, lanes),
                in_specs=vmem(5),
                out_specs=vmem(1)[0],
                scratch_shapes=[pltpu.VMEM((n, lanes), BF16), pltpu.VMEM((n, lanes), BF16), pltpu.VMEM((n, lanes), F32)],
                compiler_params=params(rows),
                name="response",
            )(back, force_t, mobility, code_d, code_a)
            if pack:
                received = exchange(velocity)
        return velocity, pressure.reshape(n, 2, loads).transpose(2, 1, 0)

    begun, over = begin(USUAL)
    usual = iterate(*begun)

    def any_permutation():
        return iterate(*begin(LARGEST)[0])

    velocity, pressure = lax.cond(over[0, 0] == 0, lambda: usual, any_permutation)
    velocity = velocity.reshape(loads, slots, 2 * width)
    return velocity, pressure


def solution(mesh):
    tiles, cols = mesh.devices.shape
    cores = Mesh(mesh.devices.reshape(tiles // 2, 2, cols), ("chip", "core", "col"))
    tile = ("chip", "core")
    return jax.shard_map(
        per_device,
        mesh=cores,
        in_specs=(
            P(None, tile, "col"),
            P(tile, None, None),
            P("col", tile, None),
            P(),
            P(tile),
        ),
        out_specs=(P("col", tile, None), P("col", None, tile)),
        check_vma=False,
    )
```

```python
import functools

import jax
import jax.numpy as jnp
from jax import lax
from jax.experimental import pallas as pl
from jax.experimental.pallas import tpu as pltpu
from jax.sharding import Mesh
from jax.sharding import PartitionSpec as P

ITERS = 2
LANES = 128
USUAL = 128
LARGEST = 1152
BF16 = jnp.bfloat16
F32 = jnp.float32
I32 = jnp.int32


def vmem(n):
    return [pl.BlockSpec(memory_space=pltpu.VMEM)] * n


def params(rows):
    return pltpu.CompilerParams(vmem_limit_bytes=(20 if rows <= 4096 else 48) * 1024 * 1024)


def dot(a, b):
    return jnp.dot(a, b, preferred_element_type=F32)


def onehot(cond):
    return jnp.where(cond, 1.0, 0.0).astype(BF16)


def turned(x):
    half = x.shape[-1] // 2
    rolled = pltpu.roll(x, half, x.ndim - 1)
    lane = lax.broadcasted_iota(I32, x.shape, x.ndim - 1)
    return jnp.where(lane < half, -rolled, rolled)


def respond(mob_ref, drive_ref, out_ref, slots, width):
    for s in range(slots):
        d = drive_ref[s * width:(s + 1) * width, :]
        t = turned(d.astype(F32)).astype(BF16)
        both = jnp.concatenate([d, t], 0)
        out_ref[s * width:(s + 1) * width, :] = dot(mob_ref[s], both).astype(BF16)


def column_of(row):
    n = row.shape[1]
    wide = [jnp.broadcast_to(row[:, i:i + LANES].astype(F32), (LANES, LANES)).T for i in range(0, n, LANES)]
    return jnp.concatenate(wide, 0)[:, :1].astype(row.dtype)


def ranks(dest_a, dest_d, groups):
    n = dest_a.shape[1]
    group = lax.broadcasted_iota(I32, (2 * groups, LANES), 0)
    before = onehot(lax.broadcasted_iota(I32, (LANES, LANES), 0) < lax.broadcasted_iota(I32, (LANES, LANES), 1))
    count = jnp.zeros((2 * groups, 1), F32)
    rank_a, rank_d = [], []
    for i in range(0, n, LANES):
        is_a = group == dest_a[:, i:i + LANES]
        is_d = group == dest_d[:, i:i + LANES] + groups
        one = jnp.where(is_a | is_d, 1.0, 0.0)
        place = dot(one.astype(BF16), before) + count
        rank_a.append(jnp.sum(jnp.where(is_a, place, 0.0), 0, keepdims=True))
        rank_d.append(jnp.sum(jnp.where(is_d, place, 0.0), 0, keepdims=True))
        count += jnp.sum(one, 1, keepdims=True)
    return jnp.concatenate(rank_a, 1).astype(I32), jnp.concatenate(rank_d, 1).astype(I32), jnp.max(count)


def own_patches(own_ref, map_ref, out_ref, slots, width):
    lane = lax.broadcasted_iota(I32, (1, LANES), 1)
    per = LANES // width
    for s in range(0, slots, per):
        row = jnp.zeros((1, LANES), I32)
        for k in range(per):
            panel = own_ref[s + k]
            found = map_ref[pl.ds(panel // per, 1), :]
            for shift in range(per):
                moved = pltpu.roll(found, ((k - shift) % per) * width, 1)
                here = (lane // width == k) & (panel % per == shift)
                row = jnp.where(here, moved, row)
        out_ref[:, s * width:s * width + LANES] = row


def aux_rows(block):
    return -(-(4 * block // LANES + 1) // 16) * 16


def capacity(block):
    return block - aux_rows(block)


def each(count, body):
    if count <= 16:
        for i in range(count):
            body(i)
    else:
        pl.loop(0, count)(body)


def at(start, size):
    if isinstance(start, int):
        return slice(start, start + size)
    return pl.ds(pl.multiple_of(start, 128), size)


def code_of(dest, rank, block, cap):
    return jnp.where(rank < cap, dest * block + rank, -1)


def pack_rows(code_row, rows, out_ref):
    n = rows.shape[0]
    step = 256

    def body(i):
        j = lax.broadcasted_iota(I32, (step, n), 0) + i * step
        out_ref[at(i * step, step), :] = dot(onehot(j == code_row), rows).astype(BF16)

    each(out_ref.shape[0] // step, body)


def to_rows(in_ref, out_ref, stage, slots, width):
    stage[...] = in_ref[...].astype(F32)
    loads = in_ref.shape[0] // slots
    for s in range(slots):
        x = stage[pl.ds(s, loads, stride=slots), :].T
        out_ref[s * width:(s + 1) * width, :] = jnp.concatenate([x[:width], x[width:]], 1).astype(BF16)


def from_rows(rows, out_ref, stage, slots, width):
    loads = out_ref.shape[0] // slots
    for s in range(slots):
        x = rows[s * width:(s + 1) * width, :].astype(F32)
        x = jnp.concatenate([x[:, :loads], x[:, loads:]], 0).T
        stage[pl.ds(s, loads, stride=slots), :] = x
    out_ref[...] = stage[...].astype(BF16)


def start_kernel(
    groups, col_tiles, slots, width, block, own_ref, map_ref, loads_ref, mob_ref,
    buf_ref, code_a_ref, code_d_ref, force_ref, vel, aux_ref, stage, patch_ref,
):
    to_rows(loads_ref, force_ref, stage, slots, width)
    own_patches(own_ref, map_ref, patch_ref, slots, width)
    pr = patch_ref[...]
    n = pr.shape[1]
    col_width = n * groups // col_tiles
    chunk = n // col_tiles
    cap = capacity(block)
    q = (pr % col_width) // chunk
    dest_a = (q % (groups // 2)) * 2 + q // (groups // 2)
    local_a = (pr // col_width) * chunk + pr % chunk
    dest_d = pr // n
    rank_a, rank_d, most = ranks(dest_a, dest_d, groups)
    code_a_row = code_of(dest_a, rank_a, block, cap)
    code_a_col = column_of(code_a_row)
    code_d_col = column_of(code_of(dest_d, rank_d, block, cap))
    code_a_ref[...] = code_of(dest_a, rank_a, cap, cap)
    code_d_ref[...] = column_of(code_of(dest_d, rank_d, cap, cap))
    respond(mob_ref, force_ref, vel, slots, width)
    pack_rows(code_a_row, vel[...], buf_ref)
    na = local_a + 1
    nd = pr % n + 1
    row16 = lax.broadcasted_iota(I32, (16, n), 0)
    va = jnp.where(row16 == 0, na // 256, jnp.where(row16 == 1, na % 256, 0)).astype(F32).astype(BF16)
    vd = jnp.where(row16 == 2, nd // 256, jnp.where(row16 == 3, nd % 256, 0)).astype(F32).astype(BF16)
    over = jnp.where(most > cap, 1.0, 0.0)

    def body(i):
        j = lax.broadcasted_iota(I32, (n, LANES), 1) + i * LANES
        aux = dot(va, onehot(j == code_a_col)) + dot(vd, onehot(j == code_d_col))
        aux_ref[i] = aux

    each(groups * block // LANES, body)
    parts = block // LANES
    rest = jnp.full((aux_rows(block) - 4 * parts, LANES), over, F32)
    for d in range(groups):
        rows = [aux_ref[d * parts + k][0:4] for k in range(parts)] + [rest]
        buf_ref[d * block + cap:(d + 1) * block, :] = jnp.concatenate(rows, 0).astype(BF16)


def index_kernel(groups, block, buf_ref, data_ref, na_ref, ndc_ref, over_ref):
    over = jnp.zeros((1, LANES), F32)
    cap = capacity(block)
    parts = block // LANES
    for d in range(groups):
        data_ref[d * cap:(d + 1) * cap, :] = buf_ref[d * block:d * block + cap, :]
        aux = buf_ref[d * block + cap:(d + 1) * block, :].astype(F32)
        for k in range(0, cap, LANES):
            size = min(LANES, cap - k)
            a = aux[k // LANES * 4:k // LANES * 4 + 4]
            to = d * cap + k
            na_ref[:, to:to + size] = ((a[0:1] * 256 + a[1:2]).astype(I32) - 1)[:, :size]
            ndc_ref[to:to + size, :] = column_of((a[2:3] * 256 + a[3:4]).astype(I32) - 1)[:size]
        over = jnp.maximum(over, aux[4 * parts:4 * parts + 1])
    over_ref[...] = over.astype(I32)


def unpack_kernel(na_ref, buf_ref, out_ref, total):
    copies, n, _ = out_ref.shape
    step = 256
    total[...] = jnp.zeros(total.shape, F32)

    def body(i):
        pick = onehot(lax.broadcasted_iota(I32, (n, step), 0) == na_ref[:, at(i * step, step)])
        total[...] += dot(pick, buf_ref[at(i * step, step), :])

    each(buf_ref.shape[0] // step, body)
    natural = total[...].astype(BF16)
    for k in range(copies):
        out_ref[k] = natural


def product_kernel(first, half_ref, z_ref, g_ref, acc_ref, out_ref, f_ref, t_ref, z_head, z_tail, sems, g_part=None, g_sems=None):
    tiles, blocks, rows, lanes = g_ref.shape
    depth = tiles * rows
    head = z_head.shape[1]
    columns = pl.ds(pl.multiple_of(half_ref[0] * depth, LANES), depth)
    parts = [(z_head, slice(0, head)), (z_tail, slice(head, z_ref.shape[1]))]
    pieces = []
    if g_part is not None:
        for i in range(blocks // 2):
            pair = slice(2 * i, 2 * i + 2)
            pieces.append(pltpu.make_async_copy(g_ref.at[:, pair], g_part.at[:, pair], g_sems.at[i]))
            if i < 2:
                pieces[i].start()
    loads = []
    for r, (z_part, out_rows) in enumerate(parts):
        loads.append(pltpu.make_async_copy(z_ref.at[:, out_rows, columns], z_part, sems.at[r]))
        loads[r].start()
    for piece in pieces[2:]:
        piece.start()
    source = g_ref if g_part is None else g_part

    def fill(i):
        if pieces:
            pieces[i].wait()
        for t in range(tiles):
            at_rows = slice(t * rows, (t + 1) * rows)
            for b in range(2):
                at_lanes = slice(b * lanes, (b + 1) * lanes)
                x = source[t, 2 * i + b]
                f_ref[i, at_rows, at_lanes] = x
                t_ref[i, at_rows, at_lanes] = turned(x.astype(F32)).astype(BF16)

    for r, (z_part, out_rows) in enumerate(parts):
        for i in range(blocks // 2):
            if r == 0 and i == 0:
                fill(0)
                fill(1)
            if i == 0:
                loads[r].wait()
            if r == 0 and 0 < i < blocks // 2 - 1:
                fill(i + 1)
            p = dot(z_part[0], f_ref[i]) + dot(z_part[1], t_ref[i])
            if first:
                out_ref[i, out_rows, :] = p
            else:
                p = (acc_ref[i, out_rows, :] + p).astype(BF16)
                out_ref[2 * i, out_rows, :] = p[:, :lanes]
                out_ref[2 * i + 1, out_rows, :] = p[:, lanes:]


def first_product_kernel(half_ref, z_ref, g_ref, out_ref, *scratch):
    product_kernel(True, half_ref, z_ref, g_ref, None, out_ref, *scratch)


def second_product_kernel(half_ref, z_ref, g_ref, acc_ref, out_ref, *scratch):
    product_kernel(False, half_ref, z_ref, g_ref, acc_ref, out_ref, *scratch)


def pressure_kernel(part_ref, ndc_ref, p_ref, buf_ref):
    total = part_ref[0].astype(F32)
    for b in range(1, part_ref.shape[0]):
        total += part_ref[b].astype(F32)
    p_ref[...] = total.astype(BF16)
    n = p_ref.shape[0]
    step = 256

    def body(i):
        pick = onehot(lax.broadcasted_iota(I32, (step, n), 1) == ndc_ref[at(i * step, step), :])
        buf_ref[at(i * step, step), :] = dot(pick, p_ref[...]).astype(BF16)

    each(buf_ref.shape[0] // step, body)


def response_kernel(slots, width, pack, buf_ref, force_ref, mob_ref, code_d_ref, code_a_ref, out_ref, drive, vel, total):
    n = force_ref.shape[0]
    step = 256
    total[...] = jnp.zeros(total.shape, F32)

    def body(i):
        j = lax.broadcasted_iota(I32, (n, step), 1) + i * step
        total[...] += dot(onehot(j == code_d_ref[...]), buf_ref[at(i * step, step), :])

    each(buf_ref.shape[0] // step, body)
    drive[...] = (force_ref[...].astype(F32) - total[...]).astype(BF16)
    if pack:
        respond(mob_ref, drive, vel, slots, width)
        pack_rows(code_a_ref[...], vel[...], out_ref)
    else:
        respond(mob_ref, drive, vel, slots, width)
        from_rows(vel, out_ref, total, slots, width)


def sds(*shape, dtype=BF16):
    return jax.ShapeDtypeStruct(shape, dtype)


def product_call(kernel, half, impedance, field, acc, stream=False):
    _, n, depth = impedance.shape
    depth //= 2
    tiles, blocks, rows, lanes = field.shape
    first = acc is None
    return pl.pallas_call(
        kernel,
        out_shape=sds(blocks // 2, n, 2 * lanes, dtype=F32) if first else sds(blocks, n, lanes),
        in_specs=[
            pl.BlockSpec(memory_space=pltpu.SMEM),
            pl.BlockSpec(memory_space=pl.ANY),
            pl.BlockSpec(memory_space=pl.ANY if stream else pltpu.VMEM),
        ] + vmem(0 if first else 1),
        out_specs=vmem(1)[0],
        scratch_shapes=[
            pltpu.VMEM((blocks // 2, depth, 2 * lanes), BF16),
            pltpu.VMEM((blocks // 2, depth, 2 * lanes), BF16),
            pltpu.VMEM((2, n // 4, depth), BF16),
            pltpu.VMEM((2, n - n // 4, depth), BF16),
            pltpu.SemaphoreType.DMA((2,)),
        ] + ([pltpu.VMEM(field.shape, BF16), pltpu.SemaphoreType.DMA((blocks // 2,))] if stream else []),
        compiler_params=params(0),
        cost_estimate=pl.CostEstimate(flops=4 * n * depth * blocks * lanes, bytes_accessed=10 * 1024 * 1024, transcendentals=0),
        name="product",
    )(half, impedance, field, *([] if first else [acc]))


def per_device(impedance, mobility, force, patch_map, ownership):
    slots, width, _ = mobility.shape
    loads = force.shape[0]
    tile = ("chip", "core")
    chips = lax.axis_size("chip")
    groups = chips * 2
    col_tiles = lax.axis_size("col")
    n = slots * width
    lanes = 2 * loads
    force_rows = force.reshape(loads * slots, 2 * width)
    core = lax.axis_index("core").astype(I32)

    def exchange(buf):
        return lax.all_to_all(buf.reshape(groups, -1, lanes), tile, 0, 0).reshape(buf.shape)

    def begin(block):
        rows = groups * block
        buf, code_a, code_d, force_t = pl.pallas_call(
            functools.partial(start_kernel, groups, col_tiles, slots, width, block),
            out_shape=(sds(rows, lanes), sds(1, n, dtype=I32), sds(n, 1, dtype=I32), sds(n, lanes)),
            in_specs=[pl.BlockSpec(memory_space=pltpu.SMEM)] + vmem(3),
            out_specs=tuple(vmem(4)),
            scratch_shapes=[
                pltpu.VMEM((n, lanes), BF16),
                pltpu.VMEM((rows // LANES, 16, LANES), F32),
                pltpu.VMEM((loads * slots, 2 * width), F32),
                pltpu.VMEM((1, n), I32),
            ],
            compiler_params=params(rows),
            name="start",
        )(ownership, patch_map.reshape(-1, LANES), force_rows, mobility)
        buf = exchange(buf)
        kept = groups * capacity(block)
        data, na, nd_col, over = pl.pallas_call(
            functools.partial(index_kernel, groups, block),
            out_shape=(sds(kept, lanes), sds(1, kept, dtype=I32), sds(kept, 1, dtype=I32), sds(1, LANES, dtype=I32)),
            in_specs=vmem(1),
            out_specs=tuple(vmem(4)),
            compiler_params=params(rows),
            name="positions",
        )(buf)
        return (data, force_t, code_a, code_d, na, nd_col), over

    def iterate(received, force_t, code_a, code_d, na, nd_col):
        rows = received.shape[0]
        for iteration in range(ITERS):
            natural = pl.pallas_call(
                unpack_kernel,
                out_shape=sds(chips, n, lanes),
                in_specs=vmem(2),
                out_specs=vmem(1)[0],
                scratch_shapes=[pltpu.VMEM((n, lanes), F32)],
                compiler_params=params(rows),
                name="unpack",
            )(na, received)
            pieces = natural.reshape(chips * col_tiles, n // col_tiles, lanes)
            mine = lax.all_to_all(pieces, ("chip", "col"), 0, 0)
            other = lax.ppermute(mine, "core", [(0, 1), (1, 0)])
            shape = (chips, col_tiles, n // col_tiles, lanes)
            acc = product_call(first_product_kernel, core[None], impedance, mine.reshape(shape), None, iteration == 0)
            part = product_call(second_product_kernel, 1 - core[None], impedance, other.reshape(shape), acc)
            part = lax.all_to_all(part, "col", 0, 0)
            pressure, out = pl.pallas_call(
                pressure_kernel,
                out_shape=(sds(n, lanes), sds(rows, lanes)),
                in_specs=vmem(2),
                out_specs=tuple(vmem(2)),
                compiler_params=params(rows),
                name="pressure",
            )(part, nd_col)
            back = exchange(out)
            pack = iteration < ITERS - 1
            velocity = pl.pallas_call(
                functools.partial(response_kernel, slots, width, pack),
                out_shape=sds(rows if pack else n, lanes),
                in_specs=vmem(5),
                out_specs=vmem(1)[0],
                scratch_shapes=[pltpu.VMEM((n, lanes), BF16), pltpu.VMEM((n, lanes), BF16), pltpu.VMEM((n, lanes), F32)],
                compiler_params=params(rows),
                name="response",
            )(back, force_t, mobility, code_d, code_a)
            if pack:
                received = exchange(velocity)
        return velocity, pressure.reshape(n, 2, loads).transpose(2, 1, 0)

    begun, over = begin(USUAL)
    usual = iterate(*begun)

    def any_permutation():
        return iterate(*begin(LARGEST)[0])

    velocity, pressure = lax.cond(over[0, 0] == 0, lambda: usual, any_permutation)
    velocity = velocity.reshape(loads, slots, 2 * width)
    return velocity, pressure


def solution(mesh):
    tiles, cols = mesh.devices.shape
    cores = Mesh(mesh.devices.reshape(tiles // 2, 2, cols), ("chip", "core", "col"))
    tile = ("chip", "core")
    return jax.shard_map(
        per_device,
        mesh=cores,
        in_specs=(
            P(None, tile, "col"),
            P(tile, None, None),
            P("col", tile, None),
            P(),
            P(tile),
        ),
        out_specs=(P("col", tile, None), P("col", None, tile)),
        check_vma=False,
    )
```

```python
import functools

import jax
import jax.numpy as jnp
from jax import lax
from jax.experimental import pallas as pl
from jax.experimental.pallas import tpu as pltpu
from jax.sharding import Mesh
from jax.sharding import PartitionSpec as P

ITERS = 2
LANES = 128
USUAL = 128
LARGEST = 1152
BF16 = jnp.bfloat16
F32 = jnp.float32
I32 = jnp.int32


def vmem(n):
    return [pl.BlockSpec(memory_space=pltpu.VMEM)] * n


def params(rows):
    return pltpu.CompilerParams(vmem_limit_bytes=(20 if rows <= 4096 else 48) * 1024 * 1024)


def dot(a, b):
    return jnp.dot(a, b, preferred_element_type=F32)


def onehot(cond):
    return jnp.where(cond, 1.0, 0.0).astype(BF16)


def turned(x):
    half = x.shape[-1] // 2
    rolled = pltpu.roll(x, half, x.ndim - 1)
    lane = lax.broadcasted_iota(I32, x.shape, x.ndim - 1)
    return jnp.where(lane < half, -rolled, rolled)


def respond(mob_ref, drive_ref, out_ref, slots, width):
    for s in range(slots):
        d = drive_ref[s * width:(s + 1) * width, :]
        t = turned(d.astype(F32)).astype(BF16)
        both = jnp.concatenate([d, t], 0)
        out_ref[s * width:(s + 1) * width, :] = dot(mob_ref[s], both).astype(BF16)


def column_of(row):
    n = row.shape[1]
    wide = [jnp.broadcast_to(row[:, i:i + LANES].astype(F32), (LANES, LANES)).T for i in range(0, n, LANES)]
    return jnp.concatenate(wide, 0)[:, :1].astype(row.dtype)


def ranks(dest_a, dest_d, groups):
    n = dest_a.shape[1]
    group = lax.broadcasted_iota(I32, (2 * groups, LANES), 0)
    before = onehot(lax.broadcasted_iota(I32, (LANES, LANES), 0) < lax.broadcasted_iota(I32, (LANES, LANES), 1))
    count = jnp.zeros((2 * groups, 1), F32)
    rank_a, rank_d = [], []
    for i in range(0, n, LANES):
        is_a = group == dest_a[:, i:i + LANES]
        is_d = group == dest_d[:, i:i + LANES] + groups
        one = jnp.where(is_a | is_d, 1.0, 0.0)
        place = dot(one.astype(BF16), before) + count
        rank_a.append(jnp.sum(jnp.where(is_a, place, 0.0), 0, keepdims=True))
        rank_d.append(jnp.sum(jnp.where(is_d, place, 0.0), 0, keepdims=True))
        count += jnp.sum(one, 1, keepdims=True)
    return jnp.concatenate(rank_a, 1).astype(I32), jnp.concatenate(rank_d, 1).astype(I32), jnp.max(count)


def own_patches(own_ref, map_ref, out_ref, slots, width):
    lane = lax.broadcasted_iota(I32, (1, LANES), 1)
    per = LANES // width
    for s in range(0, slots, per):
        row = jnp.zeros((1, LANES), I32)
        for k in range(per):
            panel = own_ref[s + k]
            found = map_ref[pl.ds(panel // per, 1), :]
            for shift in range(per):
                moved = pltpu.roll(found, ((k - shift) % per) * width, 1)
                here = (lane // width == k) & (panel % per == shift)
                row = jnp.where(here, moved, row)
        out_ref[:, s * width:s * width + LANES] = row


def aux_rows(block):
    return -(-(4 * block // LANES + 1) // 16) * 16


def capacity(block):
    return block - aux_rows(block)


def each(count, body):
    if count <= 16:
        for i in range(count):
            body(i)
    else:
        pl.loop(0, count)(body)


def at(start, size):
    if isinstance(start, int):
        return slice(start, start + size)
    return pl.ds(pl.multiple_of(start, 128), size)


def code_of(dest, rank, block, cap):
    return jnp.where(rank < cap, dest * block + rank, -1)


def pack_rows(code_row, rows, out_ref):
    n = rows.shape[0]
    step = 256

    def body(i):
        j = lax.broadcasted_iota(I32, (step, n), 0) + i * step
        out_ref[at(i * step, step), :] = dot(onehot(j == code_row), rows).astype(BF16)

    each(out_ref.shape[0] // step, body)


def to_rows(in_ref, out_ref, stage, slots, width):
    stage[...] = in_ref[...].astype(F32)
    loads = in_ref.shape[0] // slots
    for s in range(slots):
        x = stage[pl.ds(s, loads, stride=slots), :].T
        out_ref[s * width:(s + 1) * width, :] = jnp.concatenate([x[:width], x[width:]], 1).astype(BF16)


def from_rows(rows, out_ref, stage, slots, width):
    loads = out_ref.shape[0] // slots
    for s in range(slots):
        x = rows[s * width:(s + 1) * width, :].astype(F32)
        x = jnp.concatenate([x[:, :loads], x[:, loads:]], 0).T
        stage[pl.ds(s, loads, stride=slots), :] = x
    out_ref[...] = stage[...].astype(BF16)


def start_kernel(
    groups, col_tiles, slots, width, block, own_ref, map_ref, loads_ref, mob_ref,
    buf_ref, code_a_ref, code_d_ref, force_ref, vel, aux_ref, stage, patch_ref,
):
    to_rows(loads_ref, force_ref, stage, slots, width)
    own_patches(own_ref, map_ref, patch_ref, slots, width)
    pr = patch_ref[...]
    n = pr.shape[1]
    col_width = n * groups // col_tiles
    chunk = n // col_tiles
    cap = capacity(block)
    q = (pr % col_width) // chunk
    dest_a = (q % (groups // 2)) * 2 + q // (groups // 2)
    local_a = (pr // col_width) * chunk + pr % chunk
    dest_d = pr // n
    rank_a, rank_d, most = ranks(dest_a, dest_d, groups)
    code_a_row = code_of(dest_a, rank_a, block, cap)
    code_a_col = column_of(code_a_row)
    code_d_col = column_of(code_of(dest_d, rank_d, block, cap))
    code_a_ref[...] = code_of(dest_a, rank_a, cap, cap)
    code_d_ref[...] = column_of(code_of(dest_d, rank_d, cap, cap))
    respond(mob_ref, force_ref, vel, slots, width)
    pack_rows(code_a_row, vel[...], buf_ref)
    na = local_a + 1
    nd = pr % n + 1
    row16 = lax.broadcasted_iota(I32, (16, n), 0)
    va = jnp.where(row16 == 0, na // 256, jnp.where(row16 == 1, na % 256, 0)).astype(F32).astype(BF16)
    vd = jnp.where(row16 == 2, nd // 256, jnp.where(row16 == 3, nd % 256, 0)).astype(F32).astype(BF16)
    over = jnp.where(most > cap, 1.0, 0.0)

    def body(i):
        j = lax.broadcasted_iota(I32, (n, LANES), 1) + i * LANES
        aux = dot(va, onehot(j == code_a_col)) + dot(vd, onehot(j == code_d_col))
        aux_ref[i] = aux

    each(groups * block // LANES, body)
    parts = block // LANES
    rest = jnp.full((aux_rows(block) - 4 * parts, LANES), over, F32)
    for d in range(groups):
        rows = [aux_ref[d * parts + k][0:4] for k in range(parts)] + [rest]
        buf_ref[d * block + cap:(d + 1) * block, :] = jnp.concatenate(rows, 0).astype(BF16)


def index_kernel(groups, block, buf_ref, data_ref, na_ref, ndc_ref, over_ref):
    over = jnp.zeros((1, LANES), F32)
    cap = capacity(block)
    parts = block // LANES
    for d in range(groups):
        data_ref[d * cap:(d + 1) * cap, :] = buf_ref[d * block:d * block + cap, :]
        aux = buf_ref[d * block + cap:(d + 1) * block, :].astype(F32)
        for k in range(0, cap, LANES):
            size = min(LANES, cap - k)
            a = aux[k // LANES * 4:k // LANES * 4 + 4]
            to = d * cap + k
            na_ref[:, to:to + size] = ((a[0:1] * 256 + a[1:2]).astype(I32) - 1)[:, :size]
            ndc_ref[to:to + size, :] = column_of((a[2:3] * 256 + a[3:4]).astype(I32) - 1)[:size]
        over = jnp.maximum(over, aux[4 * parts:4 * parts + 1])
    over_ref[...] = over.astype(I32)


def unpack_kernel(na_ref, buf_ref, out_ref, total):
    copies, n, _ = out_ref.shape
    step = 256
    total[...] = jnp.zeros(total.shape, F32)

    def body(i):
        pick = onehot(lax.broadcasted_iota(I32, (n, step), 0) == na_ref[:, at(i * step, step)])
        total[...] += dot(pick, buf_ref[at(i * step, step), :])

    each(buf_ref.shape[0] // step, body)
    natural = total[...].astype(BF16)
    for k in range(copies):
        out_ref[k] = natural


def product_kernel(first, half_ref, z_ref, g_ref, acc_ref, out_ref, f_ref, t_ref, z_head, z_mid, z_tail, sems, g_part=None, g_sems=None):
    tiles, blocks, rows, lanes = g_ref.shape
    depth = tiles * rows
    head = z_head.shape[1]
    columns = pl.ds(pl.multiple_of(half_ref[0] * depth, LANES), depth)
    parts = [(z_head, slice(0, head)), (z_mid, slice(head, 2 * head)), (z_tail, slice(2 * head, z_ref.shape[1]))]
    pieces = []
    if g_part is not None:
        for i in range(blocks // 2):
            pair = slice(2 * i, 2 * i + 2)
            pieces.append(pltpu.make_async_copy(g_ref.at[:, pair], g_part.at[:, pair], g_sems.at[i]))
            if i < 2:
                pieces[i].start()
    loads = []
    for r, (z_part, out_rows) in enumerate(parts):
        loads.append(pltpu.make_async_copy(z_ref.at[:, out_rows, columns], z_part, sems.at[r]))
        loads[r].start()
    for piece in pieces[2:]:
        piece.start()
    source = g_ref if g_part is None else g_part

    def fill(i):
        if pieces:
            pieces[i].wait()
        for t in range(tiles):
            at_rows = slice(t * rows, (t + 1) * rows)
            for b in range(2):
                at_lanes = slice(b * lanes, (b + 1) * lanes)
                x = source[t, 2 * i + b]
                f_ref[i, at_rows, at_lanes] = x
                t_ref[i, at_rows, at_lanes] = turned(x.astype(F32)).astype(BF16)

    for r, (z_part, out_rows) in enumerate(parts):
        for i in range(blocks // 2):
            if r == 0 and i == 0:
                fill(0)
                fill(1)
            if i == 0:
                loads[r].wait()
            if r == 0 and 0 < i < blocks // 2 - 1:
                fill(i + 1)
            p = dot(z_part[0], f_ref[i]) + dot(z_part[1], t_ref[i])
            if first:
                out_ref[i, out_rows, :] = p
            else:
                p = (acc_ref[i, out_rows, :] + p).astype(BF16)
                out_ref[2 * i, out_rows, :] = p[:, :lanes]
                out_ref[2 * i + 1, out_rows, :] = p[:, lanes:]


def first_product_kernel(half_ref, z_ref, g_ref, out_ref, *scratch):
    product_kernel(True, half_ref, z_ref, g_ref, None, out_ref, *scratch)


def second_product_kernel(half_ref, z_ref, g_ref, acc_ref, out_ref, *scratch):
    product_kernel(False, half_ref, z_ref, g_ref, acc_ref, out_ref, *scratch)


def pressure_kernel(part_ref, ndc_ref, p_ref, buf_ref):
    total = part_ref[0].astype(F32)
    for b in range(1, part_ref.shape[0]):
        total += part_ref[b].astype(F32)
    p_ref[...] = total.astype(BF16)
    n = p_ref.shape[0]
    step = 256

    def body(i):
        pick = onehot(lax.broadcasted_iota(I32, (step, n), 1) == ndc_ref[at(i * step, step), :])
        buf_ref[at(i * step, step), :] = dot(pick, p_ref[...]).astype(BF16)

    each(buf_ref.shape[0] // step, body)


def response_kernel(slots, width, pack, buf_ref, force_ref, mob_ref, code_d_ref, code_a_ref, out_ref, drive, vel, total):
    n = force_ref.shape[0]
    step = 256
    total[...] = jnp.zeros(total.shape, F32)

    def body(i):
        j = lax.broadcasted_iota(I32, (n, step), 1) + i * step
        total[...] += dot(onehot(j == code_d_ref[...]), buf_ref[at(i * step, step), :])

    each(buf_ref.shape[0] // step, body)
    drive[...] = (force_ref[...].astype(F32) - total[...]).astype(BF16)
    if pack:
        respond(mob_ref, drive, vel, slots, width)
        pack_rows(code_a_ref[...], vel[...], out_ref)
    else:
        respond(mob_ref, drive, vel, slots, width)
        from_rows(vel, out_ref, total, slots, width)


def sds(*shape, dtype=BF16):
    return jax.ShapeDtypeStruct(shape, dtype)


def product_call(kernel, half, impedance, field, acc, stream=False):
    _, n, depth = impedance.shape
    depth //= 2
    tiles, blocks, rows, lanes = field.shape
    first = acc is None
    return pl.pallas_call(
        kernel,
        out_shape=sds(blocks // 2, n, 2 * lanes, dtype=F32) if first else sds(blocks, n, lanes),
        in_specs=[
            pl.BlockSpec(memory_space=pltpu.SMEM),
            pl.BlockSpec(memory_space=pl.ANY),
            pl.BlockSpec(memory_space=pl.ANY if stream else pltpu.VMEM),
        ] + vmem(0 if first else 1),
        out_specs=vmem(1)[0],
        scratch_shapes=[
            pltpu.VMEM((blocks // 2, depth, 2 * lanes), BF16),
            pltpu.VMEM((blocks // 2, depth, 2 * lanes), BF16),
            pltpu.VMEM((2, n // 4, depth), BF16),
            pltpu.VMEM((2, n // 4, depth), BF16),
            pltpu.VMEM((2, n - n // 4 * 2, depth), BF16),
            pltpu.SemaphoreType.DMA((3,)),
        ] + ([pltpu.VMEM(field.shape, BF16), pltpu.SemaphoreType.DMA((blocks // 2,))] if stream else []),
        compiler_params=params(0),
        cost_estimate=pl.CostEstimate(flops=4 * n * depth * blocks * lanes, bytes_accessed=10 * 1024 * 1024, transcendentals=0),
        name="product",
    )(half, impedance, field, *([] if first else [acc]))


def per_device(impedance, mobility, force, patch_map, ownership):
    slots, width, _ = mobility.shape
    loads = force.shape[0]
    tile = ("chip", "core")
    chips = lax.axis_size("chip")
    groups = chips * 2
    col_tiles = lax.axis_size("col")
    n = slots * width
    lanes = 2 * loads
    force_rows = force.reshape(loads * slots, 2 * width)
    core = lax.axis_index("core").astype(I32)

    def exchange(buf):
        return lax.all_to_all(buf.reshape(groups, -1, lanes), tile, 0, 0).reshape(buf.shape)

    def begin(block):
        rows = groups * block
        buf, code_a, code_d, force_t = pl.pallas_call(
            functools.partial(start_kernel, groups, col_tiles, slots, width, block),
            out_shape=(sds(rows, lanes), sds(1, n, dtype=I32), sds(n, 1, dtype=I32), sds(n, lanes)),
            in_specs=[pl.BlockSpec(memory_space=pltpu.SMEM)] + vmem(3),
            out_specs=tuple(vmem(4)),
            scratch_shapes=[
                pltpu.VMEM((n, lanes), BF16),
                pltpu.VMEM((rows // LANES, 16, LANES), F32),
                pltpu.VMEM((loads * slots, 2 * width), F32),
                pltpu.VMEM((1, n), I32),
            ],
            compiler_params=params(rows),
            name="start",
        )(ownership, patch_map.reshape(-1, LANES), force_rows, mobility)
        buf = exchange(buf)
        kept = groups * capacity(block)
        data, na, nd_col, over = pl.pallas_call(
            functools.partial(index_kernel, groups, block),
            out_shape=(sds(kept, lanes), sds(1, kept, dtype=I32), sds(kept, 1, dtype=I32), sds(1, LANES, dtype=I32)),
            in_specs=vmem(1),
            out_specs=tuple(vmem(4)),
            compiler_params=params(rows),
            name="positions",
        )(buf)
        return (data, force_t, code_a, code_d, na, nd_col), over

    def iterate(received, force_t, code_a, code_d, na, nd_col):
        rows = received.shape[0]
        for iteration in range(ITERS):
            natural = pl.pallas_call(
                unpack_kernel,
                out_shape=sds(chips, n, lanes),
                in_specs=vmem(2),
                out_specs=vmem(1)[0],
                scratch_shapes=[pltpu.VMEM((n, lanes), F32)],
                compiler_params=params(rows),
                name="unpack",
            )(na, received)
            pieces = natural.reshape(chips * col_tiles, n // col_tiles, lanes)
            mine = lax.all_to_all(pieces, ("chip", "col"), 0, 0)
            other = lax.ppermute(mine, "core", [(0, 1), (1, 0)])
            shape = (chips, col_tiles, n // col_tiles, lanes)
            acc = product_call(first_product_kernel, core[None], impedance, mine.reshape(shape), None, iteration == 0)
            part = product_call(second_product_kernel, 1 - core[None], impedance, other.reshape(shape), acc)
            part = lax.all_to_all(part, "col", 0, 0)
            pressure, out = pl.pallas_call(
                pressure_kernel,
                out_shape=(sds(n, lanes), sds(rows, lanes)),
                in_specs=vmem(2),
                out_specs=tuple(vmem(2)),
                compiler_params=params(rows),
                name="pressure",
            )(part, nd_col)
            back = exchange(out)
            pack = iteration < ITERS - 1
            velocity = pl.pallas_call(
                functools.partial(response_kernel, slots, width, pack),
                out_shape=sds(rows if pack else n, lanes),
                in_specs=vmem(5),
                out_specs=vmem(1)[0],
                scratch_shapes=[pltpu.VMEM((n, lanes), BF16), pltpu.VMEM((n, lanes), BF16), pltpu.VMEM((n, lanes), F32)],
                compiler_params=params(rows),
                name="response",
            )(back, force_t, mobility, code_d, code_a)
            if pack:
                received = exchange(velocity)
        return velocity, pressure.reshape(n, 2, loads).transpose(2, 1, 0)

    begun, over = begin(USUAL)
    usual = iterate(*begun)

    def any_permutation():
        return iterate(*begin(LARGEST)[0])

    velocity, pressure = lax.cond(over[0, 0] == 0, lambda: usual, any_permutation)
    velocity = velocity.reshape(loads, slots, 2 * width)
    return velocity, pressure


def solution(mesh):
    tiles, cols = mesh.devices.shape
    cores = Mesh(mesh.devices.reshape(tiles // 2, 2, cols), ("chip", "core", "col"))
    tile = ("chip", "core")
    return jax.shard_map(
        per_device,
        mesh=cores,
        in_specs=(
            P(None, tile, "col"),
            P(tile, None, None),
            P("col", tile, None),
            P(),
            P(tile),
        ),
        out_specs=(P("col", tile, None), P("col", None, tile)),
        check_vma=False,
    )
```
